128 devices in a mesh: section: 4 (over z_lo, core), dp: 32 (over z_hi, x, y).
Axes of the slice: x: 4, y: 4, z: 4 (z_hi: 2, z_lo: 2; z = z_hi * 2 + z_lo), core: 2. Of those that a mesh axis runs over, the one named last changes fastest.
Arguments:
- latents: bfloat16 [2, 32, 128, 3072], P(None, 'dp'), may hold values from -6 to 6
- modulation: float32 [4, 2, 32, 3, 3072], P('section', None, 'dp'), may hold values from -2 to 2
- query_key_value_weight: bfloat16 [4, 3072, 4608], P('section', None, 'dp'), may hold values from -0.109375 to 0.109375
- output_projection_weight: bfloat16 [4, 1536, 3072], P('section', None, 'dp'), may hold values from -0.15625 to 0.15625
- positions: int32 [2, 32, 128], P(None, 'dp'), may hold values from 0 to 4095, as said below
- counts: int32 [2, 32], P(None, 'dp'), may hold values from 1 to 128, as said below
Outputs:
- stash: bfloat16 [4, 2, 32, 128, 3072], P('section', None, 'dp')
The draws below stay inside these ranges and needn't reach their ends.
Inputs may be any that keep to these rules, and one draw needn't show every extreme that they name: Within a sample all 128 positions are distinct. `counts`: sample 0 of every microbatch uses all 128 slots.
All inputs are finite; a program needn't handle non-finite values.
Results may differ from the reference program's by a relative error of at most 0.039.
Values may be sent and summed in bfloat16 or wider, within the bound.
No kernel may reach another device: no remote copies, remote signals or barrier semaphores. Data moves between devices by JAX's collectives and lax.ppermute only.
A program may use at most 128 MiB of HBM per device.

```python
import jax
import jax.numpy as jnp
from jax import lax

D = 3072
HEADS = 12
HSZ = 128
GRID = 64
TOK = 128
MICRO = 2
HD = 1536
LAYERS = 4
BATCH = 32


def draw_modulation(key, part):
    key = jax.random.fold_in(key, 11)
    key_shift, key_scale, key_gate = jax.random.split(key, 3)
    shape = (LAYERS, MICRO, BATCH, 1, D)
    shift = 0.5 * jax.random.truncated_normal(key_shift, -4.0, 4.0, shape, jnp.float32)
    scale = jax.random.uniform(key_scale, shape, jnp.float32, -0.5, 1.5)
    gate = 0.5 * jax.random.truncated_normal(key_gate, -3.0, 3.0, shape, jnp.float32)
    return jnp.concatenate([shift, scale, gate], axis=3)


def draw_positions(key, part):
    key = jax.random.fold_in(key, 12)
    sample_keys = jax.random.split(key, MICRO * BATCH)
    chosen = jax.vmap(lambda one_key: jax.random.permutation(one_key, GRID * GRID)[:TOK])(sample_keys)
    return chosen.reshape(MICRO, BATCH, TOK).astype(jnp.int32)


def draw_counts(key, part):
    key = jax.random.fold_in(key, 13)
    drawn = jax.random.randint(key, (MICRO, BATCH), 1, TOK + 1)
    first = jnp.arange(BATCH, dtype=jnp.int32)[None, :] == 0
    return jnp.where(first, TOK, drawn).astype(jnp.int32)


def shard_levels(stream_key, shape, shards, smallest, high):
    def one(position, blocks):
        draws = jax.random.uniform(jax.random.fold_in(jax.random.fold_in(stream_key, 6), position), (blocks,), jnp.float32, smallest / len(shards), high / len(shards))
        return jnp.repeat(jnp.exp(draws), shape[position] // blocks).reshape((-1,) + (1,) * (len(shape) - position - 1))

    gain = one(*shards[0])
    for cut in shards[1:]:
        gain = gain * one(*cut)
    return gain


def noise(own_key, extent, deviation, bound, pieces=(), held_as=jnp.bfloat16):
    result = deviation * jax.random.normal(own_key, extent, jnp.float32)
    if pieces:
        result = result * shard_levels(own_key, extent, pieces, -0.22, 0.18)
    return jnp.clip(result, -bound, bound).astype(held_as)


def setup_inputs(seed: int = 0) -> dict:
    key_of = jax.random.split(jax.random.key(seed), 7)
    return {
        "latents": noise(key_of[0], (MICRO, BATCH, TOK, D), 1.0, 6.0, ((1, 32),)),
        "modulation": draw_modulation(jax.random.fold_in(key_of[6], 71), 0),
        "query_key_value_weight": noise(key_of[2], (LAYERS, D, 3 * HD), D ** -0.5, 0.109375, ((0, 4), (2, 32))),
        "output_projection_weight": noise(key_of[3], (LAYERS, HD, D), HD ** -0.5, 0.15625, ((0, 4), (2, 32))),
        "positions": draw_positions(jax.random.fold_in(key_of[6], 71), 0),
        "counts": draw_counts(jax.random.fold_in(key_of[6], 71), 0),
    }


def modulate(hidden_rows, modulation_rows):
    values = hidden_rows.astype(jnp.float32)
    center = lax.optimization_barrier(jnp.mean(values, axis=-1, keepdims=True))
    spread = lax.optimization_barrier(jnp.mean((values - center) ** 2, axis=-1, keepdims=True))
    normed = (values - center) / jnp.sqrt(spread + 1e-06)
    return (normed * (1.0 + modulation_rows[:, 1:2]) + modulation_rows[:, 0:1]).astype(jnp.bfloat16)

def rope_tables(patch_coordinates):
    quarter = HSZ // 4
    frequency = 10000.0 ** (-jnp.arange(quarter, dtype=jnp.float32) / quarter)
    row_coord = (patch_coordinates // GRID).astype(jnp.float32)
    col_coord = (patch_coordinates % GRID).astype(jnp.float32)
    row_angle = row_coord[..., None, None] * frequency
    col_angle = col_coord[..., None, None] * frequency
    return (jnp.cos(row_angle), jnp.sin(row_angle), jnp.cos(col_angle), jnp.sin(col_angle))

def rotate(values, cos_row, sin_row, cos_col, sin_col):
    quarter = HSZ // 4
    first_a = values[..., :quarter]
    second_a = values[..., quarter:2 * quarter]
    first_b = values[..., 2 * quarter:3 * quarter]
    second_b = values[..., 3 * quarter:]
    return jnp.concatenate([first_a * cos_row - second_a * sin_row, first_a * sin_row + second_a * cos_row, first_b * cos_col - second_b * sin_col, first_b * sin_col + second_b * cos_col], axis=-1)

def attend(qkv, patch_coordinates, active_token_count):
    samples, token_count = (qkv.shape[0], qkv.shape[1])
    sliced = qkv.reshape(samples, token_count, 3, HEADS, HSZ)
    tables = rope_tables(patch_coordinates)
    query = rotate(sliced[:, :, 0].astype(jnp.float32), *tables).astype(jnp.bfloat16)
    keys = rotate(sliced[:, :, 1].astype(jnp.float32), *tables).astype(jnp.bfloat16)
    values = sliced[:, :, 2]
    scores = jnp.einsum('bqhd,bkhd->bhqk', query.astype(jnp.float32), keys.astype(jnp.float32)) * HSZ ** (-0.5)
    live = jnp.arange(token_count, dtype=jnp.int32)[None, :] < active_token_count[:, None]
    scores = jnp.where(live[:, None, None, :], scores, -1e+30)
    row_max = lax.optimization_barrier(jnp.max(scores, axis=-1, keepdims=True))
    expd = jnp.exp(scores - row_max)
    weights = (expd / lax.optimization_barrier(jnp.sum(expd, axis=-1, keepdims=True))).astype(jnp.bfloat16)
    mixed = jnp.einsum('bhqk,bkhd->bqhd', weights.astype(jnp.float32), values.astype(jnp.float32))
    return mixed.astype(jnp.bfloat16).reshape(samples, token_count, HEADS * HSZ)

def transformer_layer_step(hidden_rows, modulation_rows, query_key_value_slice, output_weight_slice, patch_coordinates, active_token_count):
    samples, token_count, width = hidden_rows.shape
    normed = modulate(hidden_rows, modulation_rows)
    qkv = jnp.dot(normed.reshape(-1, width), query_key_value_slice, preferred_element_type=jnp.float32).astype(jnp.bfloat16)
    mixed = attend(qkv.reshape(samples, token_count, -1), patch_coordinates, active_token_count)
    proj = jnp.dot(mixed.reshape(-1, HEADS * HSZ), output_weight_slice, preferred_element_type=jnp.float32).astype(jnp.bfloat16)
    proj = proj.reshape(samples, token_count, width)
    return (hidden_rows.astype(jnp.float32) + modulation_rows[:, 2:3] * proj.astype(jnp.float32)).astype(jnp.bfloat16)

def reference(latents, modulation, query_key_value_weight, output_projection_weight, positions, counts):
    per_micro = []
    for microbatch_number in range(MICRO):
        hidden_rows = latents[microbatch_number]
        states = []
        for current_layer_number in range(LAYERS):
            hidden_rows = transformer_layer_step(hidden_rows, modulation[current_layer_number, microbatch_number], query_key_value_weight[current_layer_number], output_projection_weight[current_layer_number], positions[microbatch_number], counts[microbatch_number])
            states.append(hidden_rows)
        per_micro.append(jnp.stack([states[-1]] + states[:-1], axis=0))
    return jnp.stack(per_micro, axis=1)
```

```python
import jax
import jax.numpy as jnp
from jax import lax
from jax.experimental import pallas as pl
from jax.experimental.pallas import tpu as pltpu
from jax.sharding import Mesh
from jax.sharding import PartitionSpec as P

D = 3072
HEADS = 12
HSZ = 128
GRID = 64
TOK = 128
HD = 1536
LAYERS = 4
ROWS = 2 * TOK
QD = D // 4
QH = HD // 4
AXES = ("z_lo", "core", "z_hi", "x", "y")
RING = ("z_lo", "z_hi")
VMEM_LIMIT = 48 * 1024 * 1024
HBM = pl.BlockSpec(memory_space=pl.ANY)
SMEM = pl.BlockSpec(memory_space=pltpu.SMEM)
VMEM = pl.BlockSpec(memory_space=pltpu.VMEM)


def ring_index(z):
    return (z % 2) * 2 + z // 2


def ring_permute(value, steps):
    pairs = [(ring_index(z), ring_index((z + steps) % 4)) for z in range(4)]
    return lax.ppermute(value, RING, pairs)


def ring_gather(value):
    return [value] + [ring_permute(value, k) for k in (1, 2, 3)]


def core_swap(value):
    return lax.ppermute(value, "core", [(0, 1), (1, 0)])


def plane_permute(value, steps, phase):
    pairs = []
    for c in range(2):
        for x in range(4):
            for y in range(4):
                if (c + phase) % 2 == 0:
                    tx, ty = (x + steps) % 4, y
                else:
                    tx, ty = x, (y + steps) % 4
                pairs.append((c * 16 + x * 4 + y, c * 16 + tx * 4 + ty))
    return lax.ppermute(value, ("core", "x", "y"), pairs)


def gather_layer(shard):
    stack = jnp.stack([shard] + [plane_permute(shard, k, 0) for k in (1, 2, 3)])
    mine = [stack] + [plane_permute(stack, k, 1) for k in (1, 2, 3)]
    return mine + [core_swap(piece) for piece in mine]


def stack_ids(core, x, y):
    ids = []
    for own in (True, False):
        c = core if own else 1 - core
        for j in range(4):
            for k in range(4):
                cx = jnp.where(c == 0, x - k, x - j) % 4
                cy = jnp.where(c == 0, y - j, y - k) % 4
                ids.append((cx * 4 + cy) * 2 + c)
    return ids


def rotate(values, cosine, sine, first):
    partner = jnp.where(first, pltpu.roll(values, 96, 1), pltpu.roll(values, 32, 1))
    return (values * cosine + partner * sine).astype(jnp.bfloat16)


def attention_kernel(meta, p0, p1, p2, p3, mods, cosine, sine, *rest):
    stacks, (att, kept, w, y, sems) = rest[:8], rest[8:]
    pieces = (p0, p1, p2, p3)
    copies = []
    for b in range(8):
        for s in range(4):
            i = b * 4 + s
            row = pl.multiple_of(meta[i] * 96, 96)
            for j in range(3):
                copy = pltpu.make_async_copy(
                    stacks[b].at[s, pl.ds(96 * j, 96), :],
                    w.at[pl.ds(row, 96), pl.ds(384 * j, 384)],
                    sems.at[i * 3 + j],
                )
                copy.start()
                copies.append(copy)
    for b in range(2):
        rows = pl.ds(b * TOK, TOK)
        total = jnp.zeros((TOK, 1), jnp.float32)
        for p in pieces:
            total += jnp.sum(p[rows, :].astype(jnp.float32), axis=1, keepdims=True)
        center = total / D
        total = jnp.zeros((TOK, 1), jnp.float32)
        for p in pieces:
            total += jnp.sum((p[rows, :].astype(jnp.float32) - center) ** 2, axis=1, keepdims=True)
        inverse = 1.0 / jnp.sqrt(total / D + 1e-06)
        for k, p in enumerate(pieces):
            q = meta[32 + k]
            normed = (p[rows, :].astype(jnp.float32) - center) * inverse
            shift = mods[q, b, 0:1, :]
            scale = mods[q, b, 1:2, :]
            y[rows, pl.ds(pl.multiple_of(q * QD, QD), QD)] = (normed * (1.0 + scale) + shift).astype(jnp.bfloat16)
    keep_row = pl.multiple_of(meta[38] * TOK, TOK)
    for k, p in enumerate(pieces):
        kept[:, pl.ds(pl.multiple_of(meta[32 + k] * QD, QD), QD)] = p[pl.ds(keep_row, TOK), :]
    for copy in copies:
        copy.wait()
    qkv = jnp.dot(y[...], w[...], preferred_element_type=jnp.float32).astype(jnp.bfloat16)
    lane = lax.broadcasted_iota(jnp.int32, (TOK, HSZ), 1)
    first = (lane % 64) < 32
    for b in range(2):
        live = lane < meta[36 + b]
        lo = b * TOK
        cb, sb = cosine[lo : lo + TOK, :], sine[lo : lo + TOK, :]
        for h in range(3):
            query = rotate(qkv[lo : lo + TOK, h * HSZ : (h + 1) * HSZ].astype(jnp.float32), cb, sb, first)
            key = rotate(qkv[lo : lo + TOK, QH + h * HSZ : QH + (h + 1) * HSZ].astype(jnp.float32), cb, sb, first)
            value = qkv[lo : lo + TOK, 2 * QH + h * HSZ : 2 * QH + (h + 1) * HSZ]
            scores = lax.dot_general(query, key, (((1,), (1,)), ((), ())), preferred_element_type=jnp.float32)
            scores = jnp.where(live, scores * HSZ ** (-0.5), -1e30)
            expd = jnp.exp(scores - jnp.max(scores, axis=1, keepdims=True))
            weights = (expd / jnp.sum(expd, axis=1, keepdims=True)).astype(jnp.bfloat16)
            mixed = jnp.dot(weights, value, preferred_element_type=jnp.float32)
            att[lo : lo + TOK, h * HSZ : (h + 1) * HSZ] = mixed.astype(jnp.bfloat16)


def project_kernel(meta, a0, a1, a2, a3, hidden, gate, *rest):
    stacks, (out, w, a, sems) = rest[:8], rest[8:]
    copies = []
    for b in range(8):
        for s in range(4):
            i = b * 4 + s
            row = pl.multiple_of(meta[i] * 48, 48)
            for j in range(2):
                copy = pltpu.make_async_copy(
                    stacks[b].at[s, pl.ds(288 + 48 * j, 48), :],
                    w.at[pl.ds(row, 48), pl.ds(384 * j, 384)],
                    sems.at[i * 2 + j],
                )
                copy.start()
                copies.append(copy)
    for k, p in enumerate((a0, a1, a2, a3)):
        a[:, pl.ds(pl.multiple_of(meta[39 + k] * QH, QH), QH)] = p[...]
    for copy in copies:
        copy.wait()
    proj = jnp.dot(a[...], w[...], preferred_element_type=jnp.float32).astype(jnp.bfloat16)
    for b in range(2):
        lo = b * TOK
        out[lo : lo + TOK, :] = (
            hidden[lo : lo + TOK, :].astype(jnp.float32)
            + gate[b : b + 1, :] * proj[lo : lo + TOK, :].astype(jnp.float32)
        ).astype(jnp.bfloat16)


def attention(meta, pieces, mods, cosine, sine, stacks):
    return pl.pallas_call(
        attention_kernel,
        out_shape=(
            jax.ShapeDtypeStruct((ROWS, QH), jnp.bfloat16),
            jax.ShapeDtypeStruct((TOK, D), jnp.bfloat16),
        ),
        in_specs=[SMEM] + [VMEM] * 7 + [HBM] * 8,
        out_specs=(VMEM, VMEM),
        scratch_shapes=[
            pltpu.VMEM((D, 3 * QH), jnp.bfloat16),
            pltpu.VMEM((ROWS, D), jnp.bfloat16),
            pltpu.SemaphoreType.DMA((96,)),
        ],
        compiler_params=pltpu.CompilerParams(vmem_limit_bytes=VMEM_LIMIT),
        cost_estimate=pl.CostEstimate(flops=2 * ROWS * D * 3 * QH, bytes_accessed=10000000, transcendentals=100000),
        name="attention",
    )(meta, *pieces, mods, cosine, sine, *stacks)


def project(meta, parts, hidden, gate, stacks):
    return pl.pallas_call(
        project_kernel,
        out_shape=jax.ShapeDtypeStruct((ROWS, QD), jnp.bfloat16),
        in_specs=[SMEM] + [VMEM] * 6 + [HBM] * 8,
        out_specs=VMEM,
        scratch_shapes=[
            pltpu.VMEM((HD, QD), jnp.bfloat16),
            pltpu.VMEM((ROWS, HD), jnp.bfloat16),
            pltpu.SemaphoreType.DMA((64,)),
        ],
        compiler_params=pltpu.CompilerParams(vmem_limit_bytes=VMEM_LIMIT),
        cost_estimate=pl.CostEstimate(flops=2 * ROWS * HD * QD, bytes_accessed=4000000, transcendentals=0),
        name="project",
    )(meta, *parts, hidden, gate, *stacks)


def pick(options, index):
    return lax.dynamic_index_in_dim(jnp.stack(options), index, 0, keepdims=False)


def weight_shards(qkv_w, out_w, z_lo, core, z_hi):
    z = 2 * z_hi + z_lo
    rows = lax.all_to_all(qkv_w.reshape(16, 192, 144), ("x", "y"), 0, 0)
    rows = rows.transpose(1, 0, 2).reshape(192, HD + QD)
    outs = lax.all_to_all(out_w.reshape(16, 96, 96), ("x", "y"), 0, 0)
    outs = outs.transpose(1, 0, 2).reshape(96, HD)
    uniform = jnp.where(z_hi == 0, rows[:, :HD], rows[:, QD:])
    halves = jnp.where(z_hi == 0, rows[:, HD:], rows[:, :QD])
    uniform = uniform.reshape(192, 4, QH).transpose(1, 0, 2)
    parts = [lax.dynamic_index_in_dim(uniform, (z + k) % 4, 0, keepdims=False) for k in range(4)]
    got = jnp.stack([parts[0]] + [ring_permute(parts[k], k) for k in (1, 2, 3)])
    sources = [lax.dynamic_index_in_dim(got, (z - i) % 4, 0, keepdims=False) for i in range(4)]
    halves = halves.reshape(192, 2, QH).transpose(1, 0, 2)
    outs = outs.reshape(96, 2, 2, QH).transpose(1, 2, 0, 3).reshape(2, 192, QH)
    both = jnp.concatenate([halves, outs], axis=1)
    own = lax.dynamic_index_in_dim(both, z_lo, 0, keepdims=False)
    other = lax.ppermute(
        lax.dynamic_index_in_dim(both, 1 - z_lo, 0, keepdims=False), "z_lo", [(0, 1), (1, 0)]
    )
    layers = []
    for i in range(2):
        mixed = jnp.where(z_lo == i, own, other)
        pieces = [sources[i], mixed[:192], sources[2 + i]]
        block = jnp.stack(pieces).reshape(3, 2, 96, QH).transpose(1, 0, 2, 3).reshape(2, 288, QH)
        tail = mixed[192:].reshape(2, 2, 48, QH).transpose(1, 0, 2, 3).reshape(2, 96, QH)
        layers.append(jnp.concatenate([block, tail], axis=1))
    pair = jnp.stack(layers)
    mine = lax.dynamic_index_in_dim(pair, core, 1, keepdims=False)
    theirs = core_swap(lax.dynamic_index_in_dim(pair, 1 - core, 1, keepdims=False))
    shards = []
    for i in range(2):
        shards.append(jnp.where(core == 0, mine[i], theirs[i]))
        shards.append(jnp.where(core == 0, theirs[i], mine[i]))
    return shards


def on_device(latents, modulation, qkv_w, out_w, positions, counts):
    z_lo, core, z_hi = (lax.axis_index(a) for a in ("z_lo", "core", "z_hi"))
    x, y = lax.axis_index("x"), lax.axis_index("y")
    z = 2 * z_hi + z_lo

    small = jnp.zeros((2, 1, D), jnp.float32)
    small = lax.dynamic_update_slice(small, positions.astype(jnp.float32).reshape(2, 1, TOK), (0, 0, 0))
    small = lax.dynamic_update_slice(small, counts.astype(jnp.float32).reshape(2, 1, 1), (0, 0, TOK))
    cond = jnp.concatenate([modulation[0, :, 0], small], axis=1)
    mine = lax.dynamic_index_in_dim(cond, core, 0, keepdims=False)
    theirs = core_swap(lax.dynamic_index_in_dim(cond, 1 - core, 0, keepdims=False))
    pair = jnp.where(core == 0, jnp.stack([mine, theirs]), jnp.stack([theirs, mine]))
    ring = jnp.stack(ring_gather(pair))
    by_z = [lax.dynamic_index_in_dim(ring, (z - i) % 4, 0, keepdims=False) for i in range(4)]
    cond = jnp.stack([jnp.stack([by_z[layer // 2][layer % 2], by_z[2 + layer // 2][layer % 2]]) for layer in range(4)])
    place = cond[0, :, 3, :TOK]
    count = cond[0, :, 3, TOK].astype(jnp.int32)
    mods = cond[:, :, 0:2].reshape(4, 2, 2, 4, QD).transpose(0, 3, 1, 2, 4)
    gates = lax.dynamic_slice_in_dim(cond[:, :, 2], z * QD, QD, 2)

    patch = place.astype(jnp.int32).reshape(ROWS)
    quarter = HSZ // 4
    frequency = 10000.0 ** (-jnp.arange(quarter, dtype=jnp.float32) / quarter)
    row_angle = (patch // GRID).astype(jnp.float32)[:, None] * frequency
    col_angle = (patch % GRID).astype(jnp.float32)[:, None] * frequency
    angle = jnp.concatenate([row_angle, row_angle, col_angle, col_angle], axis=1)
    cosine = jnp.cos(angle)
    sine = jnp.sin(angle) * jnp.where(jnp.arange(HSZ) % 64 < 32, -1.0, 1.0).astype(jnp.float32)

    own = lax.dynamic_index_in_dim(latents, core, 0, keepdims=False)[0]
    pairs = [(ring_index(a), ring_index(3 - a)) for a in range(4)]
    other = lax.ppermute(own, RING, pairs)
    hidden = jnp.concatenate([jnp.where(z_hi == 0, own, other), jnp.where(z_hi == 0, other, own)], axis=0)
    pieces = [hidden[:, q * QD : (q + 1) * QD] for q in range(4)]
    quarter_of = lax.dynamic_slice_in_dim(hidden, z * QD, QD, 1)

    shards = weight_shards(qkv_w[0], out_w[0], z_lo, core, z_hi)
    ids = stack_ids(core, x, y)
    around = [(z - k) % 4 for k in range(4)]
    kept = []
    for layer in range(LAYERS):
        stacks = gather_layer(shards[layer])
        order = around if layer else [0, 1, 2, 3]
        meta = jnp.stack([jnp.asarray(v, jnp.int32) for v in ids + list(order) + [count[0], count[1], z_hi] + around])
        att, keep = attention(meta, pieces, mods[layer], cosine, sine, stacks)
        kept.append(keep)
        quarter_of = project(meta, ring_gather(att), quarter_of, gates[layer], stacks)
        if layer < LAYERS - 1:
            pieces = ring_gather(quarter_of)

    halves = quarter_of.reshape(2, TOK, QD)
    same = lax.dynamic_index_in_dim(halves, z_hi, 0, keepdims=False)
    cross = lax.dynamic_index_in_dim(halves, 1 - z_hi, 0, keepdims=False)

    def send(value, moves):
        return lax.ppermute(value, RING, [(ring_index(a), ring_index(b)) for a, b in moves])

    parts = [same, send(cross, [(1, 2), (3, 0)]), send(cross, [(0, 2), (2, 0)]), send(same, [(1, 0), (3, 2)])]
    last = jnp.concatenate([pick(parts, (z - q) % 4) for q in range(4)], axis=1)
    early = jnp.where(z_lo == 0, kept[1], kept[2])
    late = jnp.where(z_lo == 0, last, kept[3])
    stay = jnp.where(core == z_lo, late, early)
    leave = core_swap(jnp.where(core == z_lo, early, late))
    first = jnp.where(core == 0, stay, leave)
    second = jnp.where(core == 0, leave, stay)
    return jnp.stack([first, second])[None, :, None]


def solution(mesh):
    ring_mesh = Mesh(mesh.devices.reshape(2, 2, 2, 4, 4), AXES)
    section, dp = ("z_lo", "core"), ("z_hi", "x", "y")
    return jax.shard_map(
        on_device,
        mesh=ring_mesh,
        in_specs=(
            P(None, dp, None, None),
            P(section, None, dp, None, None),
            P(section, None, dp),
            P(section, None, dp),
            P(None, dp, None),
            P(None, dp),
        ),
        out_specs=P(section, None, dp, None, None),
        check_vma=False,
    )
```

```python
import functools

import jax
import jax.numpy as jnp
from jax import lax
from jax.experimental import pallas as pl
from jax.experimental.pallas import tpu as pltpu
from jax.sharding import Mesh
from jax.sharding import PartitionSpec as P

D = 3072
HEADS = 12
HSZ = 128
GRID = 64
TOK = 128
HD = 1536
LAYERS = 4
ROWS = 2 * TOK
QD = D // 4
QH = HD // 4
AXES = ("z_lo", "core", "z_hi", "x", "y")
VMEM_LIMIT = 48 * 1024 * 1024
HBM = pl.BlockSpec(memory_space=pl.ANY)
SMEM = pl.BlockSpec(memory_space=pltpu.SMEM)
VMEM = pl.BlockSpec(memory_space=pltpu.VMEM)


def device_permute(value, place):
    pairs = []
    for z in range(4):
        for c in range(2):
            target = place(z, c)
            if target is not None:
                tz, tc = target
                pairs.append(((z % 2) * 4 + c * 2 + z // 2, (tz % 2) * 4 + tc * 2 + tz // 2))
    return lax.ppermute(value, ("z_lo", "core", "z_hi"), pairs)


def ring_gather(value):
    got = [device_permute(value, lambda z, c, k=k: ((z + k) % 4, c)) for k in (1, 2, 3)]
    return [value] + got


def core_swap(value):
    return lax.ppermute(value, "core", [(0, 1), (1, 0)])


def rotate(values, cosine, sine, first):
    partner = jnp.where(first, pltpu.roll(values, 96, 1), pltpu.roll(values, 32, 1))
    return (values * cosine + partner * sine).astype(jnp.bfloat16)


def start_copies(part, weights, first, count, target, sems):
    copies = []
    for j in range(count):
        source = weights.at[:, :, part, :, pl.ds(first + 48 * j, 48), :]
        copies.append(pltpu.make_async_copy(source, target(j), sems.at[j]))
    for copy in copies:
        copy.start()
    return copies


def attention_kernel(part, meta, p0, p1, p2, p3, mods, cosine, sine, weights, att, kept, w, y, sems):
    pieces = (p0, p1, p2, p3)
    copies = start_copies(part, weights, 0, 3, lambda j: w.at[:, :, :, :, pl.ds(QH * j, QH)], sems)
    for b in range(2):
        rows = pl.ds(b * TOK, TOK)
        total = jnp.zeros((TOK, 1), jnp.float32)
        for p in pieces:
            total += jnp.sum(p[rows, :].astype(jnp.float32), axis=1, keepdims=True)
        center = total / D
        total = jnp.zeros((TOK, 1), jnp.float32)
        for p in pieces:
            total += jnp.sum((p[rows, :].astype(jnp.float32) - center) ** 2, axis=1, keepdims=True)
        inverse = 1.0 / jnp.sqrt(total / D + 1e-06)
        for k, p in enumerate(pieces):
            q = meta[k]
            normed = (p[rows, :].astype(jnp.float32) - center) * inverse
            shift = mods[q, b, 0:1, :]
            scale = mods[q, b, 1:2, :]
            y[rows, pl.ds(pl.multiple_of(q * QD, QD), QD)] = (normed * (1.0 + scale) + shift).astype(jnp.bfloat16)
    keep_row = pl.multiple_of(meta[6] * TOK, TOK)
    for k, p in enumerate(pieces):
        kept[:, pl.ds(pl.multiple_of(meta[k] * QD, QD), QD)] = p[pl.ds(keep_row, TOK), :]
    for copy in copies:
        copy.wait()
    qkv = jnp.dot(y[...], w[...].reshape(D, 3 * QH), preferred_element_type=jnp.float32).astype(jnp.bfloat16)
    lane = lax.broadcasted_iota(jnp.int32, (TOK, HSZ), 1)
    first = (lane % 64) < 32
    for b in range(2):
        live = lane < meta[4 + b]
        lo = b * TOK
        cb, sb = cosine[lo : lo + TOK, :], sine[lo : lo + TOK, :]
        for h in range(3):
            query = rotate(qkv[lo : lo + TOK, h * HSZ : (h + 1) * HSZ].astype(jnp.float32), cb, sb, first)
            key = rotate(qkv[lo : lo + TOK, QH + h * HSZ : QH + (h + 1) * HSZ].astype(jnp.float32), cb, sb, first)
            value = qkv[lo : lo + TOK, 2 * QH + h * HSZ : 2 * QH + (h + 1) * HSZ]
            scores = lax.dot_general(query, key, (((1,), (1,)), ((), ())), preferred_element_type=jnp.float32)
            scores = jnp.where(live, scores * HSZ ** (-0.5), -1e30)
            expd = jnp.exp(scores - jnp.max(scores, axis=1, keepdims=True))
            weights = (expd / jnp.sum(expd, axis=1, keepdims=True)).astype(jnp.bfloat16)
            mixed = jnp.dot(weights, value, preferred_element_type=jnp.float32)
            att[lo : lo + TOK, h * HSZ : (h + 1) * HSZ] = mixed.astype(jnp.bfloat16)


def project_kernel(part, meta, a0, a1, a2, a3, hidden, gate, weights, out, w, a, sems):
    copies = start_copies(part, weights, 144, 1, lambda j: w, sems)
    for k, p in enumerate((a0, a1, a2, a3)):
        a[:, pl.ds(pl.multiple_of(meta[7 + k] * QH, QH), QH)] = p[...]
    for copy in copies:
        copy.wait()
    for n in range(2):
        cols = pl.ds(n * QH, QH)
        proj = jnp.dot(a[...], w[n].reshape(HD, QH), preferred_element_type=jnp.float32).astype(jnp.bfloat16)
        for b in range(2):
            lo = b * TOK
            out[lo : lo + TOK, cols] = (
                hidden[lo : lo + TOK, cols].astype(jnp.float32)
                + gate[b : b + 1, cols] * proj[lo : lo + TOK, :].astype(jnp.float32)
            ).astype(jnp.bfloat16)


def attention(meta, pieces, mods, cosine, sine, weights, part):
    return pl.pallas_call(
        functools.partial(attention_kernel, part),
        out_shape=(
            jax.ShapeDtypeStruct((ROWS, QH), jnp.bfloat16),
            jax.ShapeDtypeStruct((TOK, D), jnp.bfloat16),
        ),
        in_specs=[SMEM] + [VMEM] * 7 + [HBM],
        out_specs=(VMEM, VMEM),
        scratch_shapes=[
            pltpu.VMEM((2, 16, 2, 48, 3 * QH), jnp.bfloat16),
            pltpu.VMEM((ROWS, D), jnp.bfloat16),
            pltpu.SemaphoreType.DMA((3,)),
        ],
        compiler_params=pltpu.CompilerParams(vmem_limit_bytes=VMEM_LIMIT),
        cost_estimate=pl.CostEstimate(flops=2 * ROWS * D * 3 * QH, bytes_accessed=10000000, transcendentals=100000),
        name="attention",
    )(meta, *pieces, mods, cosine, sine, weights)


def project(meta, parts, hidden, gate, weights, part):
    return pl.pallas_call(
        functools.partial(project_kernel, part),
        out_shape=jax.ShapeDtypeStruct((ROWS, QD), jnp.bfloat16),
        in_specs=[SMEM] + [VMEM] * 6 + [HBM],
        out_specs=VMEM,
        scratch_shapes=[
            pltpu.VMEM((2, 16, 2, 48, QH), jnp.bfloat16),
            pltpu.VMEM((ROWS, HD), jnp.bfloat16),
            pltpu.SemaphoreType.DMA((1,)),
        ],
        compiler_params=pltpu.CompilerParams(vmem_limit_bytes=VMEM_LIMIT),
        cost_estimate=pl.CostEstimate(flops=2 * ROWS * HD * QD, bytes_accessed=4000000, transcendentals=0),
        name="project",
    )(meta, *parts, hidden, gate, weights)


def pick(options, index):
    return lax.dynamic_index_in_dim(jnp.asarray(options), index, 0, keepdims=False)


def weight_shards(qkv_w, out_w):
    rows = qkv_w.reshape(2, 16, 2, 48, 144).transpose(2, 1, 3, 0, 4).reshape(32, 48, 288)
    outs = out_w.reshape(16, 2, 48, 96).transpose(1, 0, 2, 3).reshape(32, 48, 96)
    mixed = lax.all_to_all(jnp.concatenate([rows, outs], axis=2), ("z_hi", "x", "y"), 0, 0)
    by_core = []
    outs = mixed[:, :, 288:].transpose(1, 0, 2).reshape(48, 4, 2, QH)
    for c in range(2):
        rows = mixed[:, :, 144 * c : 144 * c + 144].transpose(1, 0, 2).reshape(48, 3, 4, QH)
        block = jnp.concatenate([rows, outs[:, None, :, c]], axis=1)
        by_core.append(block.transpose(2, 1, 0, 3).reshape(2, 2, 192, QH))
    blocks = jnp.stack(by_core, axis=2).transpose(1, 2, 0, 3, 4)
    shards = lax.all_to_all(blocks.reshape(8, 192, QH), ("z_lo", "core", "z_hi"), 0, 0)
    return shards.reshape(LAYERS, 2, 192, QH)


def on_device(latents, modulation, qkv_w, out_w, positions, counts):
    z_lo, core, z_hi = (lax.axis_index(a) for a in ("z_lo", "core", "z_hi"))
    z = 2 * z_hi + z_lo

    small = jnp.zeros((2, 1, D), jnp.float32)
    small = lax.dynamic_update_slice(small, positions.astype(jnp.float32).reshape(2, 1, TOK), (0, 0, 0))
    small = lax.dynamic_update_slice(small, counts.astype(jnp.float32).reshape(2, 1, 1), (0, 0, TOK))
    cond = jnp.concatenate([modulation[0, :, 0], small], axis=1)
    mine = lax.dynamic_index_in_dim(cond, core, 0, keepdims=False)
    theirs = core_swap(lax.dynamic_index_in_dim(cond, 1 - core, 0, keepdims=False))
    pair = jnp.where(core == 0, jnp.stack([mine, theirs]), jnp.stack([theirs, mine]))
    places = [(z - k) % 4 for k in range(4)]
    ring = jnp.stack(ring_gather(pair))
    by_z = [pick(ring, (z - i) % 4) for i in range(4)]
    cond = jnp.stack([jnp.stack([by_z[layer // 2][layer % 2], by_z[2 + layer // 2][layer % 2]]) for layer in range(4)])
    place = cond[0, :, 3, :TOK]
    count = cond[0, :, 3, TOK].astype(jnp.int32)
    mods = cond[:, :, 0:2].reshape(4, 2, 2, 4, QD).transpose(0, 3, 1, 2, 4)
    gates = lax.dynamic_slice_in_dim(cond[:, :, 2], z * QD, QD, 2)

    patch = place.astype(jnp.int32).reshape(ROWS)
    quarter = HSZ // 4
    frequency = 10000.0 ** (-jnp.arange(quarter, dtype=jnp.float32) / quarter)
    row_angle = (patch // GRID).astype(jnp.float32)[:, None] * frequency
    col_angle = (patch % GRID).astype(jnp.float32)[:, None] * frequency
    angle = jnp.concatenate([row_angle, row_angle, col_angle, col_angle], axis=1)
    cosine = jnp.cos(angle)
    sine = jnp.sin(angle) * jnp.where(jnp.arange(HSZ) % 64 < 32, -1.0, 1.0).astype(jnp.float32)

    own = lax.dynamic_index_in_dim(latents, core, 0, keepdims=False)[0]
    other = device_permute(own, lambda a, c: (3 - a, c))
    hidden = jnp.concatenate([jnp.where(z_hi == 0, own, other), jnp.where(z_hi == 0, other, own)], axis=0)
    pieces = [hidden[:, q * QD : (q + 1) * QD] for q in range(4)]
    quarter_of = lax.dynamic_slice_in_dim(hidden, z * QD, QD, 1)

    shards = weight_shards(qkv_w[0], out_w[0])
    plane = ("core", "x", "y")
    gathered = [lax.all_gather(shards[i : i + 2], plane).reshape(2, 16, 2, 2, 192, QH) for i in (0, 2)]
    weights = [(gathered[layer // 2], layer % 2) for layer in range(LAYERS)]
    kept = []
    for layer in range(LAYERS):
        order = places if layer else [0, 1, 2, 3]
        meta = jnp.stack([jnp.asarray(v, jnp.int32) for v in list(order) + [count[0], count[1], z_hi] + places])
        att, keep = attention(meta, pieces, mods[layer], cosine, sine, *weights[layer])
        kept.append(keep)
        quarter_of = project(meta, ring_gather(att), quarter_of, gates[layer], *weights[layer])
        if layer < LAYERS - 1:
            pieces = ring_gather(quarter_of)

    halves = quarter_of.reshape(2, TOK, QD)
    same = lax.dynamic_index_in_dim(halves, z_hi, 0, keepdims=False)
    cross = lax.dynamic_index_in_dim(halves, 1 - z_hi, 0, keepdims=False)

    def send(value, moves):
        return device_permute(value, lambda a, c: (moves[a], c) if a in moves else None)

    parts = [same, send(cross, {1: 2, 3: 0}), send(cross, {0: 2, 2: 0}), send(same, {1: 0, 3: 2})]
    parts = jnp.stack(parts)
    last = jnp.concatenate([pick(parts, (z - q) % 4) for q in range(4)], axis=1)
    early = jnp.where(z_lo == 0, kept[1], kept[2])
    late = jnp.where(z_lo == 0, last, kept[3])
    stay = jnp.where(core == z_lo, late, early)
    leave = core_swap(jnp.where(core == z_lo, early, late))
    first = jnp.where(core == 0, stay, leave)
    second = jnp.where(core == 0, leave, stay)
    return jnp.stack([first, second])[None, :, None]


def solution(mesh):
    ring_mesh = Mesh(mesh.devices.reshape(2, 2, 2, 4, 4), AXES)
    section, dp = ("z_lo", "core"), ("z_hi", "x", "y")
    return jax.shard_map(
        on_device,
        mesh=ring_mesh,
        in_specs=(
            P(None, dp, None, None),
            P(section, None, dp, None, None),
            P(section, None, dp),
            P(section, None, dp),
            P(None, dp, None),
            P(None, dp),
        ),
        out_specs=P(section, None, dp, None, None),
        check_vma=False,
    )
```

```python
import functools

import jax
import jax.numpy as jnp
from jax import lax
from jax.experimental import pallas as pl
from jax.experimental.pallas import tpu as pltpu
from jax.sharding import Mesh
from jax.sharding import PartitionSpec as P

D = 3072
HEADS = 12
HSZ = 128
GRID = 64
TOK = 128
HD = 1536
LAYERS = 4
ROWS = 2 * TOK
QD = D // 4
QH = HD // 4
AXES = ("z_lo", "core", "z_hi", "x", "y")
VMEM_LIMIT = 48 * 1024 * 1024
HBM = pl.BlockSpec(memory_space=pl.ANY)
SMEM = pl.BlockSpec(memory_space=pltpu.SMEM)
VMEM = pl.BlockSpec(memory_space=pltpu.VMEM)


def device_permute(value, place):
    pairs = []
    for z in range(4):
        for c in range(2):
            target = place(z, c)
            if target is not None:
                tz, tc = target
                pairs.append(((z % 2) * 4 + c * 2 + z // 2, (tz % 2) * 4 + tc * 2 + tz // 2))
    return lax.ppermute(value, ("z_lo", "core", "z_hi"), pairs)


def ring_step(value, steps):
    return device_permute(value, lambda z, c: ((z + steps) % 4, c))


def ring_gather(value):
    return [value] + [ring_step(value, k) for k in (1, 2, 3)]


def ring_gather_rows(value):
    before, after = ring_step(value, 1), ring_step(value, 3)
    return [value, before, after, ring_step(before[:TOK], 1), ring_step(after[TOK:], 3)]


def core_swap(value):
    return lax.ppermute(value, "core", [(0, 1), (1, 0)])


def rotate(values, cosine, sine, first):
    partner = jnp.where(first, pltpu.roll(values, 96, 1), pltpu.roll(values, 32, 1))
    return (values * cosine + partner * sine).astype(jnp.bfloat16)


def start_copies(weights, first, count, rows, target, sems):
    copies = [
        pltpu.make_async_copy(weights.at[:, :, :, pl.ds(first + rows * j, rows), :], target(j), sems.at[j])
        for j in range(count)
    ]
    for copy in copies:
        copy.start()
    return copies


def attention_kernel(first, meta, p0, p1, p2, p3a, p3b, mods, cosine, sine, weights, att, kept, w, y, sems):
    copies = start_copies(weights, first, 3, 48, lambda j: w.at[:, :, :, :, pl.ds(QH * j, QH)], sems)
    for b in range(2):
        rows = pl.ds(b * TOK, TOK)
        pieces = [p.at[rows] for p in (p0, p1, p2)] + [(p3a, p3b)[b]]
        total = jnp.zeros((TOK, 1), jnp.float32)
        for p in pieces:
            total += jnp.sum(p[...].astype(jnp.float32), axis=1, keepdims=True)
        center = total / D
        total = jnp.zeros((TOK, 1), jnp.float32)
        for p in pieces:
            total += jnp.sum((p[...].astype(jnp.float32) - center) ** 2, axis=1, keepdims=True)
        inverse = 1.0 / jnp.sqrt(total / D + 1e-06)
        for k, p in enumerate(pieces):
            q = meta[k]
            normed = (p[...].astype(jnp.float32) - center) * inverse
            shift = mods[q, b, 0:1, :]
            scale = mods[q, b, 1:2, :]
            y[rows, pl.ds(pl.multiple_of(q * QD, QD), QD)] = (normed * (1.0 + scale) + shift).astype(jnp.bfloat16)

        @pl.when(meta[6] == b)
        def keep(pieces=pieces):
            for k, p in enumerate(pieces):
                kept[:, pl.ds(pl.multiple_of(meta[k] * QD, QD), QD)] = p[...]

    for copy in copies:
        copy.wait()
    qkv = jnp.dot(y[...], w[...].reshape(D, 3 * QH), preferred_element_type=jnp.float32).astype(jnp.bfloat16)
    lane = lax.broadcasted_iota(jnp.int32, (TOK, HSZ), 1)
    first = (lane % 64) < 32
    for b in range(2):
        live = lane < meta[4 + b]
        lo = b * TOK
        cb, sb = cosine[lo : lo + TOK, :], sine[lo : lo + TOK, :]
        for h in range(3):
            query = rotate(qkv[lo : lo + TOK, h * HSZ : (h + 1) * HSZ].astype(jnp.float32), cb, sb, first)
            key = rotate(qkv[lo : lo + TOK, QH + h * HSZ : QH + (h + 1) * HSZ].astype(jnp.float32), cb, sb, first)
            value = qkv[lo : lo + TOK, 2 * QH + h * HSZ : 2 * QH + (h + 1) * HSZ]
            scores = lax.dot_general(query, key, (((1,), (1,)), ((), ())), preferred_element_type=jnp.float32)
            scores = jnp.where(live, scores * HSZ ** (-0.5), -1e30)
            expd = jnp.exp(scores - jnp.max(scores, axis=1, keepdims=True))
            weights = (expd / jnp.sum(expd, axis=1, keepdims=True)).astype(jnp.bfloat16)
            mixed = jnp.dot(weights, value, preferred_element_type=jnp.float32)
            att[lo : lo + TOK, h * HSZ : (h + 1) * HSZ] = mixed.astype(jnp.bfloat16)


def project_kernel(first, meta, a0, a1, a2, a3, hidden, gate, weights, out, w, a, sems):
    copies = start_copies(weights, first, 1, 48, lambda j: w, sems)
    for k, part in enumerate((a0, a1, a2, a3)):
        a[:, pl.ds(pl.multiple_of(meta[7 + k] * QH, QH), QH)] = part[...]
    for copy in copies:
        copy.wait()
    for n in range(2):
        cols = pl.ds(n * QH, QH)
        proj = jnp.dot(a[...], w[n].reshape(HD, QH), preferred_element_type=jnp.float32).astype(jnp.bfloat16)
        for b in range(2):
            lo = b * TOK
            out[lo : lo + TOK, cols] = (
                hidden[lo : lo + TOK, cols].astype(jnp.float32)
                + gate[b : b + 1, cols] * proj[lo : lo + TOK, :].astype(jnp.float32)
            ).astype(jnp.bfloat16)


def finish_kernel(meta, a0, a1, a2, a3, p0, p1, p2, p3a, p3b, gate, weights, out, w, a, sems):
    copies = []
    for q in range(4):
        copies.append(
            pltpu.make_async_copy(weights.at[:, :, pl.ds(q * 96, 96), :], w.at[q], sems.at[q])
        )
        copies[-1].start()
    for k, part in enumerate((a0, a1, a2, a3)):
        a[:, pl.ds(pl.multiple_of(meta[7 + k] * QH, QH), QH)] = part[...]
    pieces = (p0, p1, p2)
    for k in range(4):
        copies[k].wait()
    for k in range(4):
        q = meta[k]
        for n in range(2):
            cols = pl.ds(n * QH, QH)
            proj = jnp.dot(a[...], w[q, n].reshape(HD, QH), preferred_element_type=jnp.float32).astype(jnp.bfloat16)
            place = pl.ds(pl.multiple_of(q * QD + n * QH, QH), QH)
            for b in range(2):
                lo = b * TOK
                hidden = pieces[k][lo : lo + TOK, cols] if k < 3 else (p3a, p3b)[b][:, cols]
                out[lo : lo + TOK, place] = (
                    hidden.astype(jnp.float32)
                    + gate[q, b : b + 1, cols] * proj[lo : lo + TOK, :].astype(jnp.float32)
                ).astype(jnp.bfloat16)


def attention(meta, pieces, mods, cosine, sine, weights, first):
    return pl.pallas_call(
        functools.partial(attention_kernel, first),
        out_shape=(
            jax.ShapeDtypeStruct((ROWS, QH), jnp.bfloat16),
            jax.ShapeDtypeStruct((TOK, D), jnp.bfloat16),
        ),
        in_specs=[SMEM] + [VMEM] * 8 + [HBM],
        out_specs=(VMEM, VMEM),
        scratch_shapes=[
            pltpu.VMEM((2, 16, 2, 48, 3 * QH), jnp.bfloat16),
            pltpu.VMEM((ROWS, D), jnp.bfloat16),
            pltpu.SemaphoreType.DMA((3,)),
        ],
        compiler_params=pltpu.CompilerParams(vmem_limit_bytes=VMEM_LIMIT),
        cost_estimate=pl.CostEstimate(flops=2 * ROWS * D * 3 * QH, bytes_accessed=10000000, transcendentals=100000),
        name="attention",
    )(meta, *pieces, mods, cosine, sine, weights)


def project(meta, parts, hidden, gate, weights, first):
    return pl.pallas_call(
        functools.partial(project_kernel, first),
        out_shape=jax.ShapeDtypeStruct((ROWS, QD), jnp.bfloat16),
        in_specs=[SMEM] + [VMEM] * 6 + [HBM],
        out_specs=VMEM,
        scratch_shapes=[
            pltpu.VMEM((2, 16, 2, 48, QH), jnp.bfloat16),
            pltpu.VMEM((ROWS, HD), jnp.bfloat16),
            pltpu.SemaphoreType.DMA((1,)),
        ],
        compiler_params=pltpu.CompilerParams(vmem_limit_bytes=VMEM_LIMIT),
        cost_estimate=pl.CostEstimate(flops=2 * ROWS * HD * QD, bytes_accessed=4000000, transcendentals=0),
        name="project",
    )(meta, *parts, hidden, gate, weights)


def finish(meta, parts, pieces, gate, weights):
    return pl.pallas_call(
        finish_kernel,
        out_shape=jax.ShapeDtypeStruct((ROWS, D), jnp.bfloat16),
        in_specs=[SMEM] + [VMEM] * 10 + [HBM],
        out_specs=VMEM,
        scratch_shapes=[
            pltpu.VMEM((4, 2, 16, 96, QH), jnp.bfloat16),
            pltpu.VMEM((ROWS, HD), jnp.bfloat16),
            pltpu.SemaphoreType.DMA((4,)),
        ],
        compiler_params=pltpu.CompilerParams(vmem_limit_bytes=VMEM_LIMIT),
        cost_estimate=pl.CostEstimate(flops=2 * ROWS * HD * D, bytes_accessed=13000000, transcendentals=0),
        name="finish",
    )(meta, *parts, *pieces, gate, weights)


def pick(options, index):
    return lax.dynamic_index_in_dim(jnp.asarray(options), index, 0, keepdims=False)


def weight_shards(qkv_w, out_w):
    rows = qkv_w.reshape(2, 16, 2, 48, 144).transpose(2, 1, 3, 0, 4).reshape(32, 48, 288)
    outs = out_w.reshape(16, 2, 48, 96).transpose(1, 0, 2, 3).reshape(32, 48, 96)
    mixed = lax.all_to_all(jnp.concatenate([rows, outs], axis=2), ("z_hi", "x", "y"), 0, 0)
    by_core = []
    outs = mixed[:, :, 288:].transpose(1, 0, 2).reshape(48, 4, 2, QH)
    for c in range(2):
        rows = mixed[:, :, 144 * c : 144 * c + 144].transpose(1, 0, 2).reshape(48, 3, 4, QH)
        block = jnp.concatenate([rows, outs[:, None, :, c]], axis=1)
        by_core.append(block.transpose(2, 1, 0, 3).reshape(2, 2, 192, QH))
    blocks = jnp.stack(by_core, axis=2).transpose(1, 2, 0, 3, 4)
    shards = lax.all_to_all(blocks.reshape(8, 192, QH), ("z_lo", "core", "z_hi"), 0, 0)
    return shards.reshape(LAYERS, 2, 192, QH)


def on_device(latents, modulation, qkv_w, out_w, positions, counts):
    z_lo, core, z_hi = (lax.axis_index(a) for a in ("z_lo", "core", "z_hi"))
    z = 2 * z_hi + z_lo

    small = jnp.zeros((2, 1, D), jnp.float32)
    small = lax.dynamic_update_slice(small, positions.astype(jnp.float32).reshape(2, 1, TOK), (0, 0, 0))
    small = lax.dynamic_update_slice(small, counts.astype(jnp.float32).reshape(2, 1, 1), (0, 0, TOK))
    cond = jnp.concatenate([modulation[0, :, 0], small], axis=1)
    mine = lax.dynamic_index_in_dim(cond, core, 0, keepdims=False)
    theirs = core_swap(lax.dynamic_index_in_dim(cond, 1 - core, 0, keepdims=False))
    pair = jnp.where(core == 0, jnp.stack([mine, theirs]), jnp.stack([theirs, mine]))
    places = [(z - k) % 4 for k in range(4)]
    ring = jnp.stack(ring_gather(pair))
    by_z = [pick(ring, (z - i) % 4) for i in range(4)]
    cond = jnp.stack([jnp.stack([by_z[layer // 2][layer % 2], by_z[2 + layer // 2][layer % 2]]) for layer in range(4)])
    place = cond[0, :, 3, :TOK]
    count = cond[0, :, 3, TOK].astype(jnp.int32)
    mods = cond[:, :, 0:2].reshape(4, 2, 2, 4, QD).transpose(0, 3, 1, 2, 4)
    gates = lax.dynamic_slice_in_dim(cond[:3, :, 2], z * QD, QD, 2)
    last_gate = cond[3, :, 2].reshape(2, 4, QD).transpose(1, 0, 2)

    patch = place.astype(jnp.int32).reshape(ROWS)
    quarter = HSZ // 4
    frequency = 10000.0 ** (-jnp.arange(quarter, dtype=jnp.float32) / quarter)
    row_angle = (patch // GRID).astype(jnp.float32)[:, None] * frequency
    col_angle = (patch % GRID).astype(jnp.float32)[:, None] * frequency
    angle = jnp.concatenate([row_angle, row_angle, col_angle, col_angle], axis=1)
    cosine = jnp.cos(angle)
    sine = jnp.sin(angle) * jnp.where(jnp.arange(HSZ) % 64 < 32, -1.0, 1.0).astype(jnp.float32)

    own = lax.dynamic_index_in_dim(latents, core, 0, keepdims=False)[0]
    other = device_permute(own, lambda a, c: (3 - a, c))
    hidden = jnp.concatenate([jnp.where(z_hi == 0, own, other), jnp.where(z_hi == 0, other, own)], axis=0)
    pieces = [hidden[:, q * QD : (q + 1) * QD] for q in range(3)] + [hidden[:TOK, 3 * QD :], hidden[TOK:, 3 * QD :]]
    quarter_of = lax.dynamic_slice_in_dim(hidden, z * QD, QD, 1)

    shards = weight_shards(qkv_w[0], out_w[0])
    plane = ("core", "x", "y")
    front = lax.all_gather(jnp.concatenate([shards[0], shards[1]], axis=1), plane)
    middle = lax.all_gather(jnp.concatenate([shards[2], shards[3, :, :144]], axis=1), plane)
    across = lax.all_gather(shards[3, :, 144:], ("z_hi", "z_lo"))
    final = lax.all_gather(across.reshape(384, QH), plane)
    front, middle = front.reshape(2, 16, 2, 384, QH), middle.reshape(2, 16, 2, 336, QH)
    final = final.reshape(2, 16, 384, QH)
    weights = [(front, 0), (front, 192), (middle, 0), (middle, 192)]
    order = [0, 1, 2, 3]
    kept = []
    for layer in range(LAYERS):
        meta = jnp.stack([jnp.asarray(v, jnp.int32) for v in order + [count[0], count[1], z_hi] + places])
        gathered, first = weights[layer]
        att, keep = attention(meta, pieces, mods[layer], cosine, sine, gathered, first)
        kept.append(keep)
        parts = ring_gather(att)
        if layer < LAYERS - 1:
            quarter_of = project(meta, parts, quarter_of, gates[layer], gathered, first + 144)
            pieces = ring_gather_rows(quarter_of)
            order = [z, (z + 3) % 4, (z + 1) % 4, (z + 2) % 4]
    last = finish(meta, parts, pieces, last_gate, final)
    last = lax.dynamic_slice_in_dim(last, z_hi * TOK, TOK, 0)

    early = jnp.where(z_lo == 0, kept[1], kept[2])
    late = jnp.where(z_lo == 0, last, kept[3])
    stay = jnp.where(core == z_lo, late, early)
    leave = core_swap(jnp.where(core == z_lo, early, late))
    first = jnp.where(core == 0, stay, leave)
    second = jnp.where(core == 0, leave, stay)
    return jnp.stack([first, second])[None, :, None]


def solution(mesh):
    ring_mesh = Mesh(mesh.devices.reshape(2, 2, 2, 4, 4), AXES)
    section, dp = ("z_lo", "core"), ("z_hi", "x", "y")
    return jax.shard_map(
        on_device,
        mesh=ring_mesh,
        in_specs=(
            P(None, dp, None, None),
            P(section, None, dp, None, None),
            P(section, None, dp),
            P(section, None, dp),
            P(None, dp, None),
            P(None, dp),
        ),
        out_specs=P(section, None, dp, None, None),
        check_vma=False,
    )
```

```python
import functools

import jax
import jax.numpy as jnp
from jax import lax
from jax.experimental import pallas as pl
from jax.experimental.pallas import tpu as pltpu
from jax.sharding import Mesh
from jax.sharding import PartitionSpec as P

D = 3072
HEADS = 12
HSZ = 128
GRID = 64
TOK = 128
HD = 1536
LAYERS = 4
ROWS = 2 * TOK
QD = D // 4
QH = HD // 4
AXES = ("z_lo", "core", "z_hi", "x", "y")
VMEM_LIMIT = 48 * 1024 * 1024
HBM = pl.BlockSpec(memory_space=pl.ANY)
SMEM = pl.BlockSpec(memory_space=pltpu.SMEM)
VMEM = pl.BlockSpec(memory_space=pltpu.VMEM)


def device_permute(value, place):
    pairs = []
    for z in range(4):
        for c in range(2):
            target = place(z, c)
            if target is not None:
                tz, tc = target
                pairs.append(((z % 2) * 4 + c * 2 + z // 2, (tz % 2) * 4 + tc * 2 + tz // 2))
    return lax.ppermute(value, ("z_lo", "core", "z_hi"), pairs)


def ring_step(value, steps):
    return device_permute(value, lambda z, c: ((z + steps) % 4, c))


def ring_gather(value):
    return [value] + [ring_step(value, k) for k in (1, 2, 3)]


def ring_gather_rows(first, second):
    first_before, second_after = ring_step(first, 1), ring_step(second, 3)
    second_before, first_after = ring_step(second, 1), ring_step(first, 3)
    return [first, second, first_before, second_before, first_after, second_after, ring_step(first_before, 1), ring_step(second_after, 3)]


def core_swap(value):
    return lax.ppermute(value, "core", [(0, 1), (1, 0)])


def rotate(values, cosine, sine, first):
    partner = jnp.where(first, pltpu.roll(values, 96, 1), pltpu.roll(values, 32, 1))
    return (values * cosine + partner * sine).astype(jnp.bfloat16)


def start_copies(weights, first, count, rows, target, sems):
    copies = [
        pltpu.make_async_copy(weights.at[:, :, :, pl.ds(first + rows * j, rows), :], target(j), sems.at[j])
        for j in range(count)
    ]
    for copy in copies:
        copy.start()
    return copies


def attention_kernel(first, meta, *rest):
    states, (mods, cosine, sine, weights, att, kept, w, y, sems) = rest[:8], rest[8:]
    copies = start_copies(weights, first, 3, 48, lambda j: w.at[:, :, :, :, pl.ds(QH * j, QH)], sems)
    for b in range(2):
        rows = pl.ds(b * TOK, TOK)
        pieces = states[b::2]
        total = jnp.zeros((TOK, 1), jnp.float32)
        for p in pieces:
            total += jnp.sum(p[...].astype(jnp.float32), axis=1, keepdims=True)
        center = total / D
        total = jnp.zeros((TOK, 1), jnp.float32)
        for p in pieces:
            total += jnp.sum((p[...].astype(jnp.float32) - center) ** 2, axis=1, keepdims=True)
        inverse = 1.0 / jnp.sqrt(total / D + 1e-06)
        for k, p in enumerate(pieces):
            q = meta[k]
            normed = (p[...].astype(jnp.float32) - center) * inverse
            shift = mods[q, b, 0:1, :]
            scale = mods[q, b, 1:2, :]
            y[rows, pl.ds(pl.multiple_of(q * QD, QD), QD)] = (normed * (1.0 + scale) + shift).astype(jnp.bfloat16)

        @pl.when(meta[6] == b)
        def keep(pieces=pieces):
            for k, p in enumerate(pieces):
                kept[:, pl.ds(pl.multiple_of(meta[k] * QD, QD), QD)] = p[...]

    for copy in copies:
        copy.wait()
    qkv = jnp.dot(y[...], w[...].reshape(D, 3 * QH), preferred_element_type=jnp.float32).astype(jnp.bfloat16)
    lane = lax.broadcasted_iota(jnp.int32, (TOK, HSZ), 1)
    first = (lane % 64) < 32
    for b in range(2):
        live = lane < meta[4 + b]
        lo = b * TOK
        cb, sb = cosine[lo : lo + TOK, :], sine[lo : lo + TOK, :]
        for h in range(3):
            query = rotate(qkv[lo : lo + TOK, h * HSZ : (h + 1) * HSZ].astype(jnp.float32), cb, sb, first)
            key = rotate(qkv[lo : lo + TOK, QH + h * HSZ : QH + (h + 1) * HSZ].astype(jnp.float32), cb, sb, first)
            value = qkv[lo : lo + TOK, 2 * QH + h * HSZ : 2 * QH + (h + 1) * HSZ]
            scores = lax.dot_general(query, key, (((1,), (1,)), ((), ())), preferred_element_type=jnp.float32)
            scores = jnp.where(live, scores * HSZ ** (-0.5), -1e30)
            expd = jnp.exp(scores - jnp.max(scores, axis=1, keepdims=True))
            weights = (expd / jnp.sum(expd, axis=1, keepdims=True)).astype(jnp.bfloat16)
            mixed = jnp.dot(weights, value, preferred_element_type=jnp.float32)
            att[lo : lo + TOK, h * HSZ : (h + 1) * HSZ] = mixed.astype(jnp.bfloat16)


def project_kernel(first, meta, a0, a1, a2, a3, hidden0, hidden1, gate, weights, out0, out1, w, a, sems):
    copies = [pltpu.make_async_copy(weights.at[n, :, :, pl.ds(first, 48), :], w.at[n], sems.at[n]) for n in range(2)]
    for copy in copies:
        copy.start()
    for k, part in enumerate((a0, a1, a2, a3)):
        a[:, pl.ds(pl.multiple_of(meta[7 + k] * QH, QH), QH)] = part[...]
    for n in range(2):
        copies[n].wait()
        cols = pl.ds(n * QH, QH)
        proj = jnp.dot(a[...], w[n].reshape(HD, QH), preferred_element_type=jnp.float32).astype(jnp.bfloat16)
        for b, (hidden, out) in enumerate(((hidden0, out0), (hidden1, out1))):
            change = gate[b : b + 1, cols] * proj[b * TOK : (b + 1) * TOK, :].astype(jnp.float32)
            out[:, cols] = (hidden[:, cols].astype(jnp.float32) + change).astype(jnp.bfloat16)


def finish_kernel(meta, a0, a1, a2, a3, *rest):
    states, (gate, weights, out, w, a, sems) = rest[:8], rest[8:]
    copies = []
    for k, ring in enumerate((0, 1, 3, 2)):
        copies.append(pltpu.make_async_copy(weights.at[:, :, pl.ds(ring * 96, 96), :], w.at[k], sems.at[k]))
        copies[-1].start()
    for k, part in enumerate((a0, a1, a2, a3)):
        a[:, pl.ds(pl.multiple_of(meta[7 + k] * QH, QH), QH)] = part[...]
    b = meta[6]
    for k in range(4):
        copies[k].wait()
        q = meta[k]
        for n in range(2):
            cols = pl.ds(n * QH, QH)
            proj = jnp.dot(a[...], w[k, n].reshape(HD, QH), preferred_element_type=jnp.float32).astype(jnp.bfloat16)
            hidden = jnp.where(b == 0, states[2 * k][:, cols], states[2 * k + 1][:, cols])
            out[:, pl.ds(pl.multiple_of(q * QD + n * QH, QH), QH)] = (
                hidden.astype(jnp.float32) + gate[q, pl.ds(b, 1), cols] * proj.astype(jnp.float32)
            ).astype(jnp.bfloat16)


def attention(meta, pieces, mods, cosine, sine, weights, first):
    return pl.pallas_call(
        functools.partial(attention_kernel, first),
        out_shape=(
            jax.ShapeDtypeStruct((ROWS, QH), jnp.bfloat16),
            jax.ShapeDtypeStruct((TOK, D), jnp.bfloat16),
        ),
        in_specs=[SMEM] + [VMEM] * 11 + [HBM],
        out_specs=(VMEM, VMEM),
        scratch_shapes=[
            pltpu.VMEM((2, 16, 2, 48, 3 * QH), jnp.bfloat16),
            pltpu.VMEM((ROWS, D), jnp.bfloat16),
            pltpu.SemaphoreType.DMA((3,)),
        ],
        compiler_params=pltpu.CompilerParams(vmem_limit_bytes=VMEM_LIMIT),
        cost_estimate=pl.CostEstimate(flops=2 * ROWS * D * 3 * QH, bytes_accessed=10000000, transcendentals=100000),
        name="attention",
    )(meta, *pieces, mods, cosine, sine, weights)


def project(meta, parts, hidden, gate, weights, first):
    return pl.pallas_call(
        functools.partial(project_kernel, first),
        out_shape=(jax.ShapeDtypeStruct((TOK, QD), jnp.bfloat16),) * 2,
        in_specs=[SMEM] + [VMEM] * 7 + [HBM],
        out_specs=(VMEM, VMEM),
        scratch_shapes=[
            pltpu.VMEM((2, 16, 2, 48, QH), jnp.bfloat16),
            pltpu.VMEM((ROWS, HD), jnp.bfloat16),
            pltpu.SemaphoreType.DMA((2,)),
        ],
        compiler_params=pltpu.CompilerParams(vmem_limit_bytes=VMEM_LIMIT),
        cost_estimate=pl.CostEstimate(flops=2 * ROWS * HD * QD, bytes_accessed=4000000, transcendentals=0),
        name="project",
    )(meta, *parts, *hidden, gate, weights)


def finish(meta, parts, pieces, gate, weights):
    return pl.pallas_call(
        finish_kernel,
        out_shape=jax.ShapeDtypeStruct((TOK, D), jnp.bfloat16),
        in_specs=[SMEM] + [VMEM] * 13 + [HBM],
        out_specs=VMEM,
        scratch_shapes=[
            pltpu.VMEM((4, 2, 16, 96, QH), jnp.bfloat16),
            pltpu.VMEM((TOK, HD), jnp.bfloat16),
            pltpu.SemaphoreType.DMA((4,)),
        ],
        compiler_params=pltpu.CompilerParams(vmem_limit_bytes=VMEM_LIMIT),
        cost_estimate=pl.CostEstimate(flops=2 * TOK * HD * D, bytes_accessed=13000000, transcendentals=0),
        name="finish",
    )(meta, *parts, *pieces, gate, weights)


def pick(options, index):
    return lax.dynamic_index_in_dim(jnp.asarray(options), index, 0, keepdims=False)


def weight_shards(qkv_w, out_w):
    rows = qkv_w.reshape(2, 16, 2, 48, 144).transpose(2, 1, 3, 0, 4).reshape(32, 48, 288)
    outs = out_w.reshape(16, 2, 48, 96).transpose(1, 0, 2, 3).reshape(32, 48, 96)
    mixed = lax.all_to_all(jnp.concatenate([rows, outs], axis=2), ("z_hi", "x", "y"), 0, 0)
    by_core = []
    outs = mixed[:, :, 288:].transpose(1, 0, 2).reshape(48, 4, 2, QH)
    for c in range(2):
        rows = mixed[:, :, 144 * c : 144 * c + 144].transpose(1, 0, 2).reshape(48, 3, 4, QH)
        block = jnp.concatenate([rows, outs[:, None, :, c]], axis=1)
        by_core.append(block.transpose(2, 1, 0, 3).reshape(2, 2, 192, QH))
    blocks = jnp.stack(by_core, axis=2).transpose(1, 2, 0, 3, 4)
    shards = lax.all_to_all(blocks.reshape(8, 192, QH), ("z_lo", "core", "z_hi"), 0, 0)
    return shards.reshape(LAYERS, 2, 192, QH)


def on_device(latents, modulation, qkv_w, out_w, positions, counts):
    z_lo, core, z_hi = (lax.axis_index(a) for a in ("z_lo", "core", "z_hi"))
    z = 2 * z_hi + z_lo

    small = jnp.zeros((2, 1, D), jnp.float32)
    small = lax.dynamic_update_slice(small, positions.astype(jnp.float32).reshape(2, 1, TOK), (0, 0, 0))
    small = lax.dynamic_update_slice(small, counts.astype(jnp.float32).reshape(2, 1, 1), (0, 0, TOK))
    cond = jnp.concatenate([modulation[0, :, 0], small], axis=1)
    mine = lax.dynamic_index_in_dim(cond, core, 0, keepdims=False)
    theirs = core_swap(lax.dynamic_index_in_dim(cond, 1 - core, 0, keepdims=False))
    pair = jnp.where(core == 0, jnp.stack([mine, theirs]), jnp.stack([theirs, mine]))
    places = [(z - k) % 4 for k in range(4)]
    ring = jnp.stack(ring_gather(pair))
    by_z = [pick(ring, (z - i) % 4) for i in range(4)]
    cond = jnp.stack([jnp.stack([by_z[layer // 2][layer % 2], by_z[2 + layer // 2][layer % 2]]) for layer in range(4)])
    place = cond[0, :, 3, :TOK]
    count = cond[0, :, 3, TOK].astype(jnp.int32)
    mods = cond[:, :, 0:2].reshape(4, 2, 2, 4, QD).transpose(0, 3, 1, 2, 4)
    gates = lax.dynamic_slice_in_dim(cond[:3, :, 2], z * QD, QD, 2)
    last_gate = cond[3, :, 2].reshape(2, 4, QD).transpose(1, 0, 2)

    patch = place.astype(jnp.int32).reshape(ROWS)
    quarter = HSZ // 4
    frequency = 10000.0 ** (-jnp.arange(quarter, dtype=jnp.float32) / quarter)
    row_angle = (patch // GRID).astype(jnp.float32)[:, None] * frequency
    col_angle = (patch % GRID).astype(jnp.float32)[:, None] * frequency
    angle = jnp.concatenate([row_angle, row_angle, col_angle, col_angle], axis=1)
    cosine = jnp.cos(angle)
    sine = jnp.sin(angle) * jnp.where(jnp.arange(HSZ) % 64 < 32, -1.0, 1.0).astype(jnp.float32)

    own = lax.dynamic_index_in_dim(latents, core, 0, keepdims=False)[0]
    other = device_permute(own, lambda a, c: (3 - a, c))
    samples = (jnp.where(z_hi == 0, own, other), jnp.where(z_hi == 0, other, own))
    pieces = [sample[:, q * QD : (q + 1) * QD] for q in range(4) for sample in samples]
    quarter_of = [lax.dynamic_slice_in_dim(sample, z * QD, QD, 1) for sample in samples]

    shards = weight_shards(qkv_w[0], out_w[0])
    plane = ("core", "x", "y")
    front = lax.all_gather(jnp.concatenate([shards[0], shards[1]], axis=1), plane)
    middle = lax.all_gather(jnp.concatenate([shards[2], shards[3, :, :144]], axis=1), plane)
    across = jnp.stack(ring_gather(shards[3, :, 144:]))
    final = lax.all_gather(across.reshape(384, QH), plane)
    front, middle = front.reshape(2, 16, 2, 384, QH), middle.reshape(2, 16, 2, 336, QH)
    final = final.reshape(2, 16, 384, QH)
    weights = [(front, 0), (front, 192), (middle, 0), (middle, 192)]
    order = [0, 1, 2, 3]
    kept = []
    for layer in range(LAYERS):
        meta = jnp.stack([jnp.asarray(v, jnp.int32) for v in order + [count[0], count[1], z_hi] + places])
        gathered, first = weights[layer]
        att, keep = attention(meta, pieces, mods[layer], cosine, sine, gathered, first)
        kept.append(keep)
        if layer < LAYERS - 1:
            quarter_of = project(meta, ring_gather(att), quarter_of, gates[layer], gathered, first + 144)
            pieces = ring_gather_rows(*quarter_of)
            order = [z, (z + 3) % 4, (z + 1) % 4, (z + 2) % 4]

    halves = att.reshape(2, TOK, QH)
    same = lax.dynamic_index_in_dim(halves, z_hi, 0, keepdims=False)
    cross = lax.dynamic_index_in_dim(halves, 1 - z_hi, 0, keepdims=False)
    moves = [(cross, {1: 2, 3: 0}), (cross, {0: 2, 2: 0}), (same, {1: 0, 3: 2})]
    parts = [same] + [device_permute(value, lambda a, c: (move[a], c) if a in move else None) for value, move in moves]
    last = finish(meta, parts, pieces, last_gate, final)

    early = jnp.where(z_lo == 0, kept[1], kept[2])
    late = jnp.where(z_lo == 0, last, kept[3])
    stay = jnp.where(core == z_lo, late, early)
    leave = core_swap(jnp.where(core == z_lo, early, late))
    first = jnp.where(core == 0, stay, leave)
    second = jnp.where(core == 0, leave, stay)
    return jnp.stack([first, second])[None, :, None]


def solution(mesh):
    ring_mesh = Mesh(mesh.devices.reshape(2, 2, 2, 4, 4), AXES)
    section, dp = ("z_lo", "core"), ("z_hi", "x", "y")
    return jax.shard_map(
        on_device,
        mesh=ring_mesh,
        in_specs=(
            P(None, dp, None, None),
            P(section, None, dp, None, None),
            P(section, None, dp),
            P(section, None, dp),
            P(None, dp, None),
            P(None, dp),
        ),
        out_specs=P(section, None, dp, None, None),
        check_vma=False,
    )
```

```python
import functools

import jax
import jax.numpy as jnp
from jax import lax
from jax.experimental import pallas as pl
from jax.experimental.pallas import tpu as pltpu
from jax.sharding import Mesh
from jax.sharding import PartitionSpec as P

D = 3072
HEADS = 12
HSZ = 128
GRID = 64
TOK = 128
HD = 1536
LAYERS = 4
ROWS = 2 * TOK
QD = D // 4
QH = HD // 4
AXES = ("z_lo", "core", "z_hi", "x", "y")
VMEM_LIMIT = 48 * 1024 * 1024
HBM = pl.BlockSpec(memory_space=pl.ANY)
SMEM = pl.BlockSpec(memory_space=pltpu.SMEM)
VMEM = pl.BlockSpec(memory_space=pltpu.VMEM)


def device_permute(value, place):
    pairs = []
    for z in range(4):
        for c in range(2):
            target = place(z, c)
            if target is not None:
                tz, tc = target
                pairs.append(((z % 2) * 4 + c * 2 + z // 2, (tz % 2) * 4 + tc * 2 + tz // 2))
    return lax.ppermute(value, ("z_lo", "core", "z_hi"), pairs)


def ring_step(value, steps):
    return device_permute(value, lambda z, c: ((z + steps) % 4, c))


def ring_gather(value):
    return [value] + [ring_step(value, k) for k in (1, 2, 3)]


def ring_gather_rows(first, second):
    first_before, second_after = ring_step(first, 1), ring_step(second, 3)
    second_before, first_after = ring_step(second, 1), ring_step(first, 3)
    return [first, second, first_before, second_before, first_after, second_after, ring_step(first_before, 1), ring_step(second_after, 3)]


def core_swap(value):
    return lax.ppermute(value, "core", [(0, 1), (1, 0)])


def rotate(values, cosine, sine, first):
    partner = jnp.where(first, pltpu.roll(values, 96, 1), pltpu.roll(values, 32, 1))
    return (values * cosine + partner * sine).astype(jnp.bfloat16)


def start_copies(weights, first, count, rows, target, sems):
    copies = [
        pltpu.make_async_copy(weights.at[:, :, :, pl.ds(first + rows * j, rows), :], target(j), sems.at[j])
        for j in range(count)
    ]
    for copy in copies:
        copy.start()
    return copies


def attention_kernel(first, meta, *rest):
    states, (mods, cosine, sine, weights, att, kept, w, y, sems) = rest[:8], rest[8:]
    copies = start_copies(weights, first, 3, 48, lambda j: w.at[:, :, :, :, pl.ds(QH * j, QH)], sems)
    for b in range(2):
        rows = pl.ds(b * TOK, TOK)
        pieces = states[b::2]
        total = jnp.zeros((TOK, 1), jnp.float32)
        for p in pieces:
            total += jnp.sum(p[...].astype(jnp.float32), axis=1, keepdims=True)
        center = total / D
        total = jnp.zeros((TOK, 1), jnp.float32)
        for p in pieces:
            total += jnp.sum((p[...].astype(jnp.float32) - center) ** 2, axis=1, keepdims=True)
        inverse = 1.0 / jnp.sqrt(total / D + 1e-06)
        for k, p in enumerate(pieces):
            q = meta[k]
            normed = (p[...].astype(jnp.float32) - center) * inverse
            shift = mods[q, b, 0:1, :]
            scale = mods[q, b, 1:2, :]
            y[rows, pl.ds(pl.multiple_of(q * QD, QD), QD)] = (normed * (1.0 + scale) + shift).astype(jnp.bfloat16)

        @pl.when(meta[6] == b)
        def keep(pieces=pieces):
            for k, p in enumerate(pieces):
                kept[:, pl.ds(pl.multiple_of(meta[k] * QD, QD), QD)] = p[...]

    for copy in copies:
        copy.wait()
    qkv = jnp.dot(y[...], w[...].reshape(D, 3 * QH), preferred_element_type=jnp.float32).astype(jnp.bfloat16)
    lane = lax.broadcasted_iota(jnp.int32, (TOK, HSZ), 1)
    first = (lane % 64) < 32
    for b in range(2):
        live = lane < meta[4 + b]
        lo = b * TOK
        cb, sb = cosine[lo : lo + TOK, :], sine[lo : lo + TOK, :]
        for h in range(3):
            query = rotate(qkv[lo : lo + TOK, h * HSZ : (h + 1) * HSZ].astype(jnp.float32), cb, sb, first)
            key = rotate(qkv[lo : lo + TOK, QH + h * HSZ : QH + (h + 1) * HSZ].astype(jnp.float32), cb, sb, first)
            value = qkv[lo : lo + TOK, 2 * QH + h * HSZ : 2 * QH + (h + 1) * HSZ]
            scores = lax.dot_general(query, key, (((1,), (1,)), ((), ())), preferred_element_type=jnp.float32)
            scores = jnp.where(live, scores * HSZ ** (-0.5), -1e30)
            expd = jnp.exp(scores - jnp.max(scores, axis=1, keepdims=True))
            weights = (expd / jnp.sum(expd, axis=1, keepdims=True)).astype(jnp.bfloat16)
            mixed = jnp.dot(weights, value, preferred_element_type=jnp.float32)
            att[lo : lo + TOK, h * HSZ : (h + 1) * HSZ] = mixed.astype(jnp.bfloat16)


def fetch_kernel(start, weights, out, sem):
    copy = pltpu.make_async_copy(weights.at[:, :, :, pl.ds(start, 48), :], out, sem)
    copy.start()
    copy.wait()


def fetch(weights, start, after):
    weights, _ = lax.optimization_barrier((weights, after))
    return pl.pallas_call(
        functools.partial(fetch_kernel, start),
        out_shape=jax.ShapeDtypeStruct((2, 16, 2, 48, QH), jnp.bfloat16),
        in_specs=[HBM],
        out_specs=VMEM,
        scratch_shapes=[pltpu.SemaphoreType.DMA],
        compiler_params=pltpu.CompilerParams(vmem_limit_bytes=VMEM_LIMIT),
        cost_estimate=pl.CostEstimate(flops=0, bytes_accessed=5000000, transcendentals=0),
        name="fetch",
    )(weights)


def project_kernel(meta, a0, a1, a2, a3, hidden0, hidden1, gate, w, out0, out1, a):
    for k, part in enumerate((a0, a1, a2, a3)):
        a[:, pl.ds(pl.multiple_of(meta[7 + k] * QH, QH), QH)] = part[...]
    for n in range(2):
        cols = pl.ds(n * QH, QH)
        proj = jnp.dot(a[...], w[n].reshape(HD, QH), preferred_element_type=jnp.float32).astype(jnp.bfloat16)
        for b, (hidden, out) in enumerate(((hidden0, out0), (hidden1, out1))):
            change = gate[b : b + 1, cols] * proj[b * TOK : (b + 1) * TOK, :].astype(jnp.float32)
            out[:, cols] = (hidden[:, cols].astype(jnp.float32) + change).astype(jnp.bfloat16)


def finish_kernel(meta, a0, a1, a2, a3, *rest):
    states, (gate, weights, out, w, a, sems) = rest[:8], rest[8:]
    copies = []
    for k, ring in enumerate((0, 1, 3, 2)):
        copies.append(pltpu.make_async_copy(weights.at[:, :, :, pl.ds(ring * 48, 48), :], w.at[k], sems.at[k]))
        copies[-1].start()
    for k, part in enumerate((a0, a1, a2, a3)):
        a[:, pl.ds(pl.multiple_of(meta[7 + k] * QH, QH), QH)] = part[...]
    b = meta[6]
    for k in range(4):
        copies[k].wait()
        q = meta[k]
        for n in range(2):
            cols = pl.ds(n * QH, QH)
            proj = jnp.dot(a[...], w[k, n].reshape(HD, QH), preferred_element_type=jnp.float32).astype(jnp.bfloat16)
            hidden = jnp.where(b == 0, states[2 * k][:, cols], states[2 * k + 1][:, cols])
            out[:, pl.ds(pl.multiple_of(q * QD + n * QH, QH), QH)] = (
                hidden.astype(jnp.float32) + gate[q, pl.ds(b, 1), cols] * proj.astype(jnp.float32)
            ).astype(jnp.bfloat16)


def attention(meta, pieces, mods, cosine, sine, weights, first):
    return pl.pallas_call(
        functools.partial(attention_kernel, first),
        out_shape=(
            jax.ShapeDtypeStruct((ROWS, QH), jnp.bfloat16),
            jax.ShapeDtypeStruct((TOK, D), jnp.bfloat16),
        ),
        in_specs=[SMEM] + [VMEM] * 11 + [HBM],
        out_specs=(VMEM, VMEM),
        scratch_shapes=[
            pltpu.VMEM((2, 16, 2, 48, 3 * QH), jnp.bfloat16),
            pltpu.VMEM((ROWS, D), jnp.bfloat16),
            pltpu.SemaphoreType.DMA((3,)),
        ],
        compiler_params=pltpu.CompilerParams(vmem_limit_bytes=VMEM_LIMIT),
        cost_estimate=pl.CostEstimate(flops=2 * ROWS * D * 3 * QH, bytes_accessed=10000000, transcendentals=100000),
        name="attention",
    )(meta, *pieces, mods, cosine, sine, weights)


def project(meta, parts, hidden, gate, weights):
    return pl.pallas_call(
        project_kernel,
        out_shape=(jax.ShapeDtypeStruct((TOK, QD), jnp.bfloat16),) * 2,
        in_specs=[SMEM] + [VMEM] * 8,
        out_specs=(VMEM, VMEM),
        scratch_shapes=[pltpu.VMEM((ROWS, HD), jnp.bfloat16)],
        compiler_params=pltpu.CompilerParams(vmem_limit_bytes=VMEM_LIMIT),
        cost_estimate=pl.CostEstimate(flops=2 * ROWS * HD * QD, bytes_accessed=4000000, transcendentals=0),
        name="project",
    )(meta, *parts, *hidden, gate, weights)


def finish(meta, parts, pieces, gate, weights):
    return pl.pallas_call(
        finish_kernel,
        out_shape=jax.ShapeDtypeStruct((TOK, D), jnp.bfloat16),
        in_specs=[SMEM] + [VMEM] * 13 + [HBM],
        out_specs=VMEM,
        scratch_shapes=[
            pltpu.VMEM((4, 2, 16, 2, 48, QH), jnp.bfloat16),
            pltpu.VMEM((TOK, HD), jnp.bfloat16),
            pltpu.SemaphoreType.DMA((4,)),
        ],
        compiler_params=pltpu.CompilerParams(vmem_limit_bytes=VMEM_LIMIT),
        cost_estimate=pl.CostEstimate(flops=2 * TOK * HD * D, bytes_accessed=13000000, transcendentals=0),
        name="finish",
    )(meta, *parts, *pieces, gate, weights)


def pick(options, index):
    return lax.dynamic_index_in_dim(jnp.asarray(options), index, 0, keepdims=False)


def pack_kernel(qkv, outs, packed):
    qkv, outs = qkv[...].T, outs[...].T
    for d in range(32):
        z_hi, plane = d // 16, d % 16
        first, second, last = (2 * plane + z_hi) * 48, (2 * plane + z_hi + 32) * 48, (2 * plane + z_hi) * 48
        packed[d] = jnp.concatenate([qkv[first : first + 48], qkv[second : second + 48], outs[last : last + 48]], axis=1)


def regroup_kernel(mixed, blocks):
    outs = jnp.concatenate([mixed[d, :, 288:384] for d in range(32)], axis=1)
    for c in range(2):
        rows = jnp.concatenate([mixed[d, :, 144 * c : 144 * c + 144] for d in range(32)], axis=1)
        for z in range(4):
            target = (z % 2) * 4 + c * 2 + z // 2
            for j in range(3):
                blocks[target, 48 * j : 48 * j + 48, :] = rows[:, HD * j + QH * z : HD * j + QH * (z + 1)]
            blocks[target, 144:, :] = outs[:, QD * z + QH * c : QD * z + QH * (c + 1)]


def weight_shards(qkv_w, out_w):
    params = pltpu.CompilerParams(vmem_limit_bytes=VMEM_LIMIT)
    packed = pl.pallas_call(
        pack_kernel,
        out_shape=jax.ShapeDtypeStruct((32, 48, 384), jnp.bfloat16),
        compiler_params=params,
        name="pack",
    )(qkv_w.T, out_w.T)
    mixed = lax.all_to_all(packed, ("z_hi", "x", "y"), 0, 0)
    blocks = pl.pallas_call(
        regroup_kernel,
        out_shape=jax.ShapeDtypeStruct((8, 192, QH), jnp.bfloat16),
        compiler_params=params,
        name="regroup",
    )(mixed)
    shards = lax.all_to_all(blocks, ("z_lo", "core", "z_hi"), 0, 0)
    return shards.reshape(LAYERS, 2, 192, QH)


def on_device(latents, modulation, qkv_w, out_w, positions, counts):
    z_lo, core, z_hi = (lax.axis_index(a) for a in ("z_lo", "core", "z_hi"))
    z = 2 * z_hi + z_lo

    small = jnp.zeros((2, 1, D), jnp.float32)
    small = lax.dynamic_update_slice(small, positions.astype(jnp.float32).reshape(2, 1, TOK), (0, 0, 0))
    small = lax.dynamic_update_slice(small, counts.astype(jnp.float32).reshape(2, 1, 1), (0, 0, TOK))
    cond = jnp.concatenate([modulation[0, :, 0], small], axis=1)
    mine = lax.dynamic_index_in_dim(cond, core, 0, keepdims=False)
    theirs = core_swap(lax.dynamic_index_in_dim(cond, 1 - core, 0, keepdims=False))
    pair = jnp.where(core == 0, jnp.stack([mine, theirs]), jnp.stack([theirs, mine]))
    places = [(z - k) % 4 for k in range(4)]
    ring = jnp.stack(ring_gather(pair))
    by_z = [pick(ring, (z - i) % 4) for i in range(4)]
    cond = jnp.stack([jnp.stack([by_z[layer // 2][layer % 2], by_z[2 + layer // 2][layer % 2]]) for layer in range(4)])
    place = cond[0, :, 3, :TOK]
    count = cond[0, :, 3, TOK].astype(jnp.int32)
    mods = cond[:, :, 0:2].reshape(4, 2, 2, 4, QD).transpose(0, 3, 1, 2, 4)
    gates = lax.dynamic_slice_in_dim(cond[:3, :, 2], z * QD, QD, 2)
    last_gate = cond[3, :, 2].reshape(2, 4, QD).transpose(1, 0, 2)

    patch = place.astype(jnp.int32).reshape(ROWS)
    quarter = HSZ // 4
    frequency = 10000.0 ** (-jnp.arange(quarter, dtype=jnp.float32) / quarter)
    row_angle = (patch // GRID).astype(jnp.float32)[:, None] * frequency
    col_angle = (patch % GRID).astype(jnp.float32)[:, None] * frequency
    angle = jnp.concatenate([row_angle, row_angle, col_angle, col_angle], axis=1)
    cosine = jnp.cos(angle)
    sine = jnp.sin(angle) * jnp.where(jnp.arange(HSZ) % 64 < 32, -1.0, 1.0).astype(jnp.float32)

    own = lax.dynamic_index_in_dim(latents, core, 0, keepdims=False)[0]
    other = device_permute(own, lambda a, c: (3 - a, c))
    samples = (jnp.where(z_hi == 0, own, other), jnp.where(z_hi == 0, other, own))
    pieces = [sample[:, q * QD : (q + 1) * QD] for q in range(4) for sample in samples]
    quarter_of = [lax.dynamic_slice_in_dim(sample, z * QD, QD, 1) for sample in samples]

    shards = weight_shards(qkv_w[0], out_w[0])
    plane = ("core", "x", "y")
    front = lax.all_gather(jnp.concatenate([shards[0], shards[1]], axis=1), plane)
    middle = lax.all_gather(jnp.concatenate([shards[2], shards[3, :, :144]], axis=1), plane)
    across = jnp.concatenate(ring_gather(shards[3, :, 144:]), axis=1)
    final = lax.all_gather(across, plane)
    front, middle = front.reshape(2, 16, 2, 384, QH), middle.reshape(2, 16, 2, 336, QH)
    final = final.reshape(2, 16, 2, 192, QH)
    weights = [(front, 0), (front, 192), (middle, 0), (middle, 192)]
    order = [0, 1, 2, 3]
    kept = []
    for layer in range(LAYERS):
        meta = jnp.stack([jnp.asarray(v, jnp.int32) for v in order + [count[0], count[1], z_hi] + places])
        gathered, first = weights[layer]
        att, keep = attention(meta, pieces, mods[layer], cosine, sine, gathered, first)
        kept.append(keep)
        if layer < LAYERS - 1:
            quarter_of = project(meta, ring_gather(att), quarter_of, gates[layer], fetch(gathered, first + 144, att))
            pieces = ring_gather_rows(*quarter_of)
            order = [z, (z + 3) % 4, (z + 1) % 4, (z + 2) % 4]

    halves = att.reshape(2, TOK, QH)
    same = lax.dynamic_index_in_dim(halves, z_hi, 0, keepdims=False)
    cross = lax.dynamic_index_in_dim(halves, 1 - z_hi, 0, keepdims=False)
    moves = [(cross, {1: 2, 3: 0}), (cross, {0: 2, 2: 0}), (same, {1: 0, 3: 2})]
    parts = [same] + [device_permute(value, lambda a, c: (move[a], c) if a in move else None) for value, move in moves]
    last = finish(meta, parts, pieces, last_gate, final)

    early = jnp.where(z_lo == 0, kept[1], kept[2])
    late = jnp.where(z_lo == 0, last, kept[3])
    stay = jnp.where(core == z_lo, late, early)
    leave = core_swap(jnp.where(core == z_lo, early, late))
    first = jnp.where(core == 0, stay, leave)
    second = jnp.where(core == 0, leave, stay)
    return jnp.stack([first, second])[None, :, None]


def solution(mesh):
    ring_mesh = Mesh(mesh.devices.reshape(2, 2, 2, 4, 4), AXES)
    section, dp = ("z_lo", "core"), ("z_hi", "x", "y")
    return jax.shard_map(
        on_device,
        mesh=ring_mesh,
        in_specs=(
            P(None, dp, None, None),
            P(section, None, dp, None, None),
            P(section, None, dp),
            P(section, None, dp),
            P(None, dp, None),
            P(None, dp),
        ),
        out_specs=P(section, None, dp, None, None),
        check_vma=False,
    )
```

```python
import functools

import jax
import jax.numpy as jnp
from jax import lax
from jax.experimental import pallas as pl
from jax.experimental.pallas import tpu as pltpu
from jax.sharding import Mesh
from jax.sharding import PartitionSpec as P

D = 3072
HEADS = 12
HSZ = 128
GRID = 64
TOK = 128
HD = 1536
LAYERS = 4
ROWS = 2 * TOK
QD = D // 4
QH = HD // 4
AXES = ("z_lo", "core", "z_hi", "x", "y")
VMEM_LIMIT = 48 * 1024 * 1024
HBM = pl.BlockSpec(memory_space=pl.ANY)
SMEM = pl.BlockSpec(memory_space=pltpu.SMEM)
VMEM = pl.BlockSpec(memory_space=pltpu.VMEM)


def device_permute(value, place):
    pairs = []
    for z in range(4):
        for c in range(2):
            target = place(z, c)
            if target is not None:
                tz, tc = target
                pairs.append(((z % 2) * 4 + c * 2 + z // 2, (tz % 2) * 4 + tc * 2 + tz // 2))
    return lax.ppermute(value, ("z_lo", "core", "z_hi"), pairs)


def ring_step(value, steps):
    return device_permute(value, lambda z, c: ((z + steps) % 4, c))


def ring_gather(value):
    return [value] + [ring_step(value, k) for k in (1, 2, 3)]


def ring_gather_rows(first, second):
    first_before, second_after = ring_step(first, 1), ring_step(second, 3)
    second_before, first_after = ring_step(second, 1), ring_step(first, 3)
    return [first, second, first_before, second_before, first_after, second_after, ring_step(first_before, 1), ring_step(second_after, 3)]


def core_swap(value):
    return lax.ppermute(value, "core", [(0, 1), (1, 0)])


def rotate(values, cosine, sine, first):
    partner = jnp.where(first, pltpu.roll(values, 96, 1), pltpu.roll(values, 32, 1))
    return (values * cosine + partner * sine).astype(jnp.bfloat16)


def attention_kernel(first, keeps, last, meta, *rest):
    states, (mods, cosine, sine, weights), outs, (w, y, both, sems, keep_sem) = rest[:8], rest[8:12], rest[12:-5], rest[-5:]
    if keeps:
        kept = outs[-1]
        for b in range(2):

            @pl.when(meta[6] == b)
            def keep(pieces=states[b::2]):
                for k, p in enumerate(pieces):
                    place = pl.ds(pl.multiple_of(meta[k] * QD, QD), QD)
                    pltpu.make_async_copy(p, kept.at[:, place], keep_sem).start()

    for i in range(4):
        core, plane = i // 2, pl.ds(i % 2 * 8, 8)
        for j in range(3):
            source = weights.at[core, plane, :, pl.ds(first + 48 * j, 48), :]
            pltpu.make_async_copy(source, w.at[i, :, :, :, pl.ds(QH * j, QH)], sems.at[i]).start()
    for b in range(2):
        rows = pl.ds(b * TOK, TOK)
        pieces = states[b::2]
        total = jnp.zeros((TOK, 1), jnp.float32)
        for p in pieces:
            total += jnp.sum(p[...].astype(jnp.float32), axis=1, keepdims=True)
        center = total / D
        total = jnp.zeros((TOK, 1), jnp.float32)
        for p in pieces:
            total += jnp.sum((p[...].astype(jnp.float32) - center) ** 2, axis=1, keepdims=True)
        inverse = 1.0 / jnp.sqrt(total / D + 1e-06)
        for k, p in enumerate(pieces):
            q = meta[k]
            normed = (p[...].astype(jnp.float32) - center) * inverse
            shift = mods[q, b, 0:1, :]
            scale = mods[q, b, 1:2, :]
            y[rows, pl.ds(pl.multiple_of(q * QD, QD), QD)] = (normed * (1.0 + scale) + shift).astype(jnp.bfloat16)

    total = jnp.zeros((ROWS, 3 * QH), jnp.float32)
    for i in range(4):
        pltpu.make_async_copy(w.at[i], w.at[i], sems.at[i]).wait()
        total += jnp.dot(y[:, i * QD : (i + 1) * QD], w[i].reshape(QD, 3 * QH), preferred_element_type=jnp.float32)
    qkv = total.astype(jnp.bfloat16)
    lane = lax.broadcasted_iota(jnp.int32, (TOK, HSZ), 1)
    first = (lane % 64) < 32
    for b in range(2):
        live = lane < meta[4 + b]
        lo = b * TOK
        cb, sb = cosine[lo : lo + TOK, :], sine[lo : lo + TOK, :]
        for h in range(3):
            query = rotate(qkv[lo : lo + TOK, h * HSZ : (h + 1) * HSZ].astype(jnp.float32), cb, sb, first)
            key = rotate(qkv[lo : lo + TOK, QH + h * HSZ : QH + (h + 1) * HSZ].astype(jnp.float32), cb, sb, first)
            value = qkv[lo : lo + TOK, 2 * QH + h * HSZ : 2 * QH + (h + 1) * HSZ]
            scores = lax.dot_general(query, key, (((1,), (1,)), ((), ())), preferred_element_type=jnp.float32)
            scores = jnp.where(live, scores * HSZ ** (-0.5), -1e30)
            expd = jnp.exp(scores - jnp.max(scores, axis=1, keepdims=True))
            weights = (expd / jnp.sum(expd, axis=1, keepdims=True)).astype(jnp.bfloat16)
            mixed = jnp.dot(weights, value, preferred_element_type=jnp.float32)
            mixed = mixed.astype(jnp.bfloat16)
            cols = pl.ds(h * HSZ, HSZ)
            if last:
                both[b, :, cols] = mixed
            else:
                outs[0][lo : lo + TOK, cols] = mixed
    if last:
        outs[0][...] = both[meta[6]]
        outs[1][...] = both[1 - meta[6]]
    if keeps:
        pltpu.make_async_copy(kept, kept, keep_sem).wait()


def fetch_kernel(start, weights, out, sem):
    copy = pltpu.make_async_copy(weights.at[:, :, :, pl.ds(start, 48), :], out, sem)
    copy.start()
    copy.wait()


def fetch(weights, start, after):
    weights, _ = lax.optimization_barrier((weights, after))
    return pl.pallas_call(
        functools.partial(fetch_kernel, start),
        out_shape=jax.ShapeDtypeStruct((2, 16, 2, 48, QH), jnp.bfloat16),
        in_specs=[HBM],
        out_specs=VMEM,
        scratch_shapes=[pltpu.SemaphoreType.DMA],
        compiler_params=pltpu.CompilerParams(vmem_limit_bytes=VMEM_LIMIT),
        cost_estimate=pl.CostEstimate(flops=0, bytes_accessed=5000000, transcendentals=0),
        name="fetch",
    )(weights)


def project_kernel(meta, a0, a1, a2, a3, hidden0, hidden1, gate, w, out0, out1, a):
    for k, part in enumerate((a0, a1, a2, a3)):
        a[:, pl.ds(pl.multiple_of(meta[7 + k] * QH, QH), QH)] = part[...]
    for n in range(2):
        cols = pl.ds(n * QH, QH)
        proj = jnp.dot(a[...], w[n].reshape(HD, QH), preferred_element_type=jnp.float32).astype(jnp.bfloat16)
        for b, (hidden, out) in enumerate(((hidden0, out0), (hidden1, out1))):
            change = gate[b : b + 1, cols] * proj[b * TOK : (b + 1) * TOK, :].astype(jnp.float32)
            out[:, cols] = (hidden[:, cols].astype(jnp.float32) + change).astype(jnp.bfloat16)


def finish_kernel(meta, a0, a1, a2, a3, *rest):
    states, (gate, weights, kept1, kept2, stay, leave, w, a, early, sems) = rest[:8], rest[8:]
    copies = []
    for k, ring in enumerate((0, 1, 3, 2)):
        copies.append(pltpu.make_async_copy(weights.at[:, :, :, pl.ds(ring * 48, 48), :], w.at[k], sems.at[k]))
        copies[-1].start()
    for z_lo, kept in enumerate((kept1, kept2)):

        @pl.when(meta[11] == z_lo)
        def bring(kept=kept):
            pltpu.make_async_copy(kept, early, sems.at[4]).start()

    for k, part in enumerate((a0, a1, a2, a3)):
        a[:, pl.ds(pl.multiple_of(meta[7 + k] * QH, QH), QH)] = part[...]
    pltpu.make_async_copy(kept1, early, sems.at[4]).wait()
    b = meta[6]
    for k in range(4):
        copies[k].wait()
        q = meta[k]
        for n in range(2):
            cols = pl.ds(n * QH, QH)
            proj = jnp.dot(a[...], w[k, n].reshape(HD, QH), preferred_element_type=jnp.float32).astype(jnp.bfloat16)
            hidden = jnp.where(b == 0, states[2 * k][:, cols], states[2 * k + 1][:, cols])
            change = gate[q, pl.ds(b, 1), cols] * proj.astype(jnp.float32)
            place = pl.ds(pl.multiple_of(q * QD + n * QH, QH), QH)
            late = jnp.where(meta[11] == 0, (hidden.astype(jnp.float32) + change).astype(jnp.bfloat16), hidden)
            stay[:, place] = jnp.where(meta[11] == meta[12], late, early[:, place])
            leave[:, place] = jnp.where(meta[11] == meta[12], early[:, place], late)


def attention(meta, pieces, mods, cosine, sine, weights, first, keeps, last):
    if last:
        attended = (jax.ShapeDtypeStruct((TOK, QH), jnp.bfloat16),) * 2
    else:
        attended = (jax.ShapeDtypeStruct((ROWS, QH), jnp.bfloat16),)
    return pl.pallas_call(
        functools.partial(attention_kernel, first, keeps, last),
        out_shape=attended + (jax.ShapeDtypeStruct((TOK, D), jnp.bfloat16),) * keeps,
        in_specs=[SMEM] + [VMEM] * 11 + [HBM],
        out_specs=(VMEM,) * len(attended) + (HBM,) * keeps,
        scratch_shapes=[
            pltpu.VMEM((4, 8, 2, 48, 3 * QH), jnp.bfloat16),
            pltpu.VMEM((ROWS, D), jnp.bfloat16),
            pltpu.VMEM((2, TOK, QH), jnp.bfloat16),
            pltpu.SemaphoreType.DMA((4,)),
            pltpu.SemaphoreType.DMA,
        ],
        compiler_params=pltpu.CompilerParams(vmem_limit_bytes=VMEM_LIMIT),
        cost_estimate=pl.CostEstimate(flops=2 * ROWS * D * 3 * QH, bytes_accessed=10000000, transcendentals=100000),
        name="attention",
    )(meta, *pieces, mods, cosine, sine, weights)


def project(meta, parts, hidden, gate, weights):
    return pl.pallas_call(
        project_kernel,
        out_shape=(jax.ShapeDtypeStruct((TOK, QD), jnp.bfloat16),) * 2,
        in_specs=[SMEM] + [VMEM] * 8,
        out_specs=(VMEM, VMEM),
        scratch_shapes=[pltpu.VMEM((ROWS, HD), jnp.bfloat16)],
        compiler_params=pltpu.CompilerParams(vmem_limit_bytes=VMEM_LIMIT),
        cost_estimate=pl.CostEstimate(flops=2 * ROWS * HD * QD, bytes_accessed=4000000, transcendentals=0),
        name="project",
    )(meta, *parts, *hidden, gate, weights)


def finish(meta, parts, pieces, gate, weights, kept):
    return pl.pallas_call(
        finish_kernel,
        out_shape=(jax.ShapeDtypeStruct((TOK, D), jnp.bfloat16),) * 2,
        in_specs=[SMEM] + [VMEM] * 13 + [HBM] * 3,
        out_specs=(VMEM, VMEM),
        scratch_shapes=[
            pltpu.VMEM((4, 2, 16, 2, 48, QH), jnp.bfloat16),
            pltpu.VMEM((TOK, HD), jnp.bfloat16),
            pltpu.VMEM((TOK, D), jnp.bfloat16),
            pltpu.SemaphoreType.DMA((5,)),
        ],
        compiler_params=pltpu.CompilerParams(vmem_limit_bytes=VMEM_LIMIT),
        cost_estimate=pl.CostEstimate(flops=2 * TOK * HD * D, bytes_accessed=13000000, transcendentals=0),
        name="finish",
    )(meta, *parts, *pieces, gate, weights, *kept)


def pick(options, index):
    return lax.dynamic_index_in_dim(jnp.asarray(options), index, 0, keepdims=False)


def pack_kernel(qkv, outs, packed):
    qkv, outs = qkv[...].T, outs[...].T
    for d in range(32):
        z_hi, plane = d // 16, d % 16
        first, second, last = (2 * plane + z_hi) * 48, (2 * plane + z_hi + 32) * 48, (2 * plane + z_hi) * 48
        packed[d] = jnp.concatenate([qkv[first : first + 48], qkv[second : second + 48], outs[last : last + 48]], axis=1)


def regroup_kernel(mixed, blocks):
    outs = jnp.concatenate([mixed[d, :, 288:384] for d in range(32)], axis=1)
    for c in range(2):
        rows = jnp.concatenate([mixed[d, :, 144 * c : 144 * c + 144] for d in range(32)], axis=1)
        for z in range(4):
            target = (z % 2) * 4 + c * 2 + z // 2
            for j in range(3):
                blocks[target, 48 * j : 48 * j + 48, :] = rows[:, HD * j + QH * z : HD * j + QH * (z + 1)]
            blocks[target, 144:, :] = outs[:, QD * z + QH * c : QD * z + QH * (c + 1)]


def weight_shards(qkv_w, out_w):
    params = pltpu.CompilerParams(vmem_limit_bytes=VMEM_LIMIT)
    packed = pl.pallas_call(
        pack_kernel,
        out_shape=jax.ShapeDtypeStruct((32, 48, 384), jnp.bfloat16),
        compiler_params=params,
        name="pack",
    )(qkv_w.T, out_w.T)
    mixed = lax.all_to_all(packed, ("z_hi", "x", "y"), 0, 0)
    blocks = pl.pallas_call(
        regroup_kernel,
        out_shape=jax.ShapeDtypeStruct((8, 192, QH), jnp.bfloat16),
        compiler_params=params,
        name="regroup",
    )(mixed)
    shards = lax.all_to_all(blocks, ("z_lo", "core", "z_hi"), 0, 0)
    return shards.reshape(LAYERS, 2, 192, QH)


def on_device(latents, modulation, qkv_w, out_w, positions, counts):
    z_lo, core, z_hi = (lax.axis_index(a) for a in ("z_lo", "core", "z_hi"))
    z = 2 * z_hi + z_lo

    small = jnp.zeros((2, 1, D), jnp.float32)
    small = lax.dynamic_update_slice(small, positions.astype(jnp.float32).reshape(2, 1, TOK), (0, 0, 0))
    small = lax.dynamic_update_slice(small, counts.astype(jnp.float32).reshape(2, 1, 1), (0, 0, TOK))
    cond = jnp.concatenate([modulation[0, :, 0], small], axis=1)
    mine = lax.dynamic_index_in_dim(cond, core, 0, keepdims=False)
    theirs = core_swap(lax.dynamic_index_in_dim(cond, 1 - core, 0, keepdims=False))
    pair = jnp.where(core == 0, jnp.stack([mine, theirs]), jnp.stack([theirs, mine]))
    places = [(z - k) % 4 for k in range(4)]
    ring = jnp.stack(ring_gather(pair))
    by_z = [pick(ring, (z - i) % 4) for i in range(4)]
    cond = jnp.stack([jnp.stack([by_z[layer // 2][layer % 2], by_z[2 + layer // 2][layer % 2]]) for layer in range(4)])
    place = cond[0, :, 3, :TOK]
    count = cond[0, :, 3, TOK].astype(jnp.int32)
    mods = cond[:, :, 0:2].reshape(4, 2, 2, 4, QD).transpose(0, 3, 1, 2, 4)
    gates = lax.dynamic_slice_in_dim(cond[:3, :, 2], z * QD, QD, 2)
    last_gate = cond[3, :, 2].reshape(2, 4, QD).transpose(1, 0, 2)

    patch = place.astype(jnp.int32).reshape(ROWS)
    quarter = HSZ // 4
    frequency = 10000.0 ** (-jnp.arange(quarter, dtype=jnp.float32) / quarter)
    row_angle = (patch // GRID).astype(jnp.float32)[:, None] * frequency
    col_angle = (patch % GRID).astype(jnp.float32)[:, None] * frequency
    angle = jnp.concatenate([row_angle, row_angle, col_angle, col_angle], axis=1)
    cosine = jnp.cos(angle)
    sine = jnp.sin(angle) * jnp.where(jnp.arange(HSZ) % 64 < 32, -1.0, 1.0).astype(jnp.float32)

    own = lax.dynamic_index_in_dim(latents, core, 0, keepdims=False)[0]
    other = device_permute(own, lambda a, c: (3 - a, c))
    samples = (jnp.where(z_hi == 0, own, other), jnp.where(z_hi == 0, other, own))
    pieces = [sample[:, q * QD : (q + 1) * QD] for q in range(4) for sample in samples]
    quarter_of = [lax.dynamic_slice_in_dim(sample, z * QD, QD, 1) for sample in samples]

    shards = weight_shards(qkv_w[0], out_w[0])
    plane = ("core", "x", "y")
    front = lax.all_gather(jnp.concatenate([shards[0], shards[1]], axis=1), plane)
    middle = lax.all_gather(jnp.concatenate([shards[2], shards[3, :, :144]], axis=1), plane)
    across = jnp.concatenate(ring_gather(shards[3, :, 144:]), axis=1)
    final = lax.all_gather(across, plane)
    front, middle = front.reshape(2, 16, 2, 384, QH), middle.reshape(2, 16, 2, 336, QH)
    final = final.reshape(2, 16, 2, 192, QH)
    weights = [(front, 0), (front, 192), (middle, 0), (middle, 192)]
    order = [0, 1, 2, 3]
    kept = []
    for layer in range(LAYERS):
        meta = jnp.stack([jnp.asarray(v, jnp.int32) for v in order + [count[0], count[1], z_hi] + places + [z_lo, core]])
        gathered, first = weights[layer]
        att = attention(meta, pieces, mods[layer], cosine, sine, gathered, first, layer in (1, 2), layer == LAYERS - 1)
        if layer in (1, 2):
            *att, keep = att
            kept.append(keep)
        if layer < LAYERS - 1:
            quarter_of = project(meta, ring_gather(att[0]), quarter_of, gates[layer], fetch(gathered, first + 144, att[0]))
            pieces = ring_gather_rows(*quarter_of)
            order = [z, (z + 3) % 4, (z + 1) % 4, (z + 2) % 4]

    same, cross = att
    moves = [(cross, {1: 2, 3: 0}), (cross, {0: 2, 2: 0}), (same, {1: 0, 3: 2})]
    parts = [same] + [device_permute(value, lambda a, c: (move[a], c) if a in move else None) for value, move in moves]
    stay, leave = finish(meta, parts, pieces, last_gate, final, kept)
    leave = core_swap(leave)
    first = jnp.where(core == 0, stay, leave)
    second = jnp.where(core == 0, leave, stay)
    return jnp.stack([first, second])[None, :, None]


def solution(mesh):
    ring_mesh = Mesh(mesh.devices.reshape(2, 2, 2, 4, 4), AXES)
    section, dp = ("z_lo", "core"), ("z_hi", "x", "y")
    return jax.shard_map(
        on_device,
        mesh=ring_mesh,
        in_specs=(
            P(None, dp, None, None),
            P(section, None, dp, None, None),
            P(section, None, dp),
            P(section, None, dp),
            P(None, dp, None),
            P(None, dp),
        ),
        out_specs=P(section, None, dp, None, None),
        check_vma=False,
    )
```

```python
import functools

import jax
import jax.numpy as jnp
from jax import lax
from jax.experimental import pallas as pl
from jax.experimental.pallas import tpu as pltpu
from jax.sharding import Mesh
from jax.sharding import PartitionSpec as P

D = 3072
HEADS = 12
HSZ = 128
GRID = 64
TOK = 128
HD = 1536
LAYERS = 4
ROWS = 2 * TOK
QD = D // 4
QH = HD // 4
AXES = ("z_lo", "core", "z_hi", "x", "y")
VMEM_LIMIT = 48 * 1024 * 1024
HBM = pl.BlockSpec(memory_space=pl.ANY)
VMEM = pl.BlockSpec(memory_space=pltpu.VMEM)


def device_permute(value, place):
    pairs = []
    for z in range(4):
        for c in range(2):
            target = place(z, c)
            if target is not None:
                tz, tc = target
                pairs.append(((z % 2) * 4 + c * 2 + z // 2, (tz % 2) * 4 + tc * 2 + tz // 2))
    return lax.ppermute(value, ("z_lo", "core", "z_hi"), pairs)


def ring_step(value, steps):
    return device_permute(value, lambda z, c: ((z + steps) % 4, c))


def ring_gather(value):
    return [value] + [ring_step(value, k) for k in (1, 2, 3)]


def ring_gather_rows(first, second):
    first_before, second_after = ring_step(first, 1), ring_step(second, 3)
    second_before, first_after = ring_step(second, 1), ring_step(first, 3)
    return [first, second, first_before, second_before, first_after, second_after, ring_step(first_before, 1), ring_step(second_after, 3)]


def core_swap(value):
    return lax.ppermute(value, "core", [(0, 1), (1, 0)])


def rotate(values, cosine, sine, first):
    partner = jnp.where(first, pltpu.roll(values, 96, 1), pltpu.roll(values, 32, 1))
    return (values * cosine + partner * sine).astype(jnp.bfloat16)


def places():
    z_lo, core, z_hi = (lax.axis_index(a) for a in ("z_lo", "core", "z_hi"))
    z = 2 * z_hi + z_lo
    around = [lax.rem(z + k, 4) for k in (0, 3, 2, 1)]
    return z_lo, core, z_hi, around, [around[0], around[1], around[3], around[2]]


def attention_kernel(first, keeps, last, *rest):
    _, _, z_hi, _, order = places()
    if not (keeps or last):
        order = [0, 1, 2, 3]
    states, (mods, tables, weights), outs, (w, y, both, sems, keep_sem) = rest[:8], rest[8:11], rest[11:-5], rest[-5:]
    if keeps:
        kept = outs[-1]
        for b in range(2):

            @pl.when(z_hi == b)
            def keep(pieces=states[b::2]):
                for k, p in enumerate(pieces):
                    place = pl.ds(pl.multiple_of(order[k] * QD, QD), QD)
                    pltpu.make_async_copy(p, kept.at[:, place], keep_sem).start()

    for i in range(4):
        core, plane = i // 2, pl.ds(i % 2 * 8, 8)
        for j in range(3):
            source = weights.at[core, plane, :, pl.ds(first + 48 * j, 48), :]
            pltpu.make_async_copy(source, w.at[i, :, :, :, pl.ds(QH * j, QH)], sems.at[i]).start()
    for b in range(2):
        rows = pl.ds(b * TOK, TOK)
        pieces = states[b::2]
        total = jnp.zeros((TOK, 1), jnp.float32)
        for p in pieces:
            total += jnp.sum(p[...].astype(jnp.float32), axis=1, keepdims=True)
        center = total / D
        total = jnp.zeros((TOK, 1), jnp.float32)
        for p in pieces:
            total += jnp.sum((p[...].astype(jnp.float32) - center) ** 2, axis=1, keepdims=True)
        inverse = 1.0 / jnp.sqrt(total / D + 1e-06)
        for k, p in enumerate(pieces):
            q = order[k]
            normed = (p[...].astype(jnp.float32) - center) * inverse
            shift = mods[q, b, 0:1, :]
            scale = mods[q, b, 1:2, :]
            y[rows, pl.ds(pl.multiple_of(q * QD, QD), QD)] = (normed * (1.0 + scale) + shift).astype(jnp.bfloat16)

    total = jnp.zeros((ROWS, 3 * QH), jnp.float32)
    for i in range(4):
        pltpu.make_async_copy(w.at[i], w.at[i], sems.at[i]).wait()
        total += jnp.dot(y[:, i * QD : (i + 1) * QD], w[i].reshape(QD, 3 * QH), preferred_element_type=jnp.float32)
    qkv = total.astype(jnp.bfloat16)
    lane = lax.broadcasted_iota(jnp.int32, (TOK, HSZ), 1)
    first = (lane % 64) < 32
    for b in range(2):
        lo = b * TOK
        cb, sb, live = tables[0, lo : lo + TOK, :], tables[1, lo : lo + TOK, :], tables[2, lo : lo + TOK, :] > 0.0
        for h in range(3):
            query = rotate(qkv[lo : lo + TOK, h * HSZ : (h + 1) * HSZ].astype(jnp.float32), cb, sb, first)
            key = rotate(qkv[lo : lo + TOK, QH + h * HSZ : QH + (h + 1) * HSZ].astype(jnp.float32), cb, sb, first)
            value = qkv[lo : lo + TOK, 2 * QH + h * HSZ : 2 * QH + (h + 1) * HSZ]
            scores = lax.dot_general(query, key, (((1,), (1,)), ((), ())), preferred_element_type=jnp.float32)
            scores = jnp.where(live, scores * HSZ ** (-0.5), -1e30)
            expd = jnp.exp(scores - jnp.max(scores, axis=1, keepdims=True))
            weights = (expd / jnp.sum(expd, axis=1, keepdims=True)).astype(jnp.bfloat16)
            mixed = jnp.dot(weights, value, preferred_element_type=jnp.float32)
            mixed = mixed.astype(jnp.bfloat16)
            cols = pl.ds(h * HSZ, HSZ)
            if last:
                both[b, :, cols] = mixed
            else:
                outs[0][lo : lo + TOK, cols] = mixed
    if last:
        outs[0][...] = both[z_hi]
        outs[1][...] = both[1 - z_hi]
    if keeps:
        pltpu.make_async_copy(kept, kept, keep_sem).wait()


def fetch_kernel(start, weights, out, sem):
    copy = pltpu.make_async_copy(weights.at[:, :, :, pl.ds(start, 48), :], out, sem)
    copy.start()
    copy.wait()


def fetch(weights, start, after):
    weights, _ = lax.optimization_barrier((weights, after))
    return pl.pallas_call(
        functools.partial(fetch_kernel, start),
        out_shape=jax.ShapeDtypeStruct((2, 16, 2, 48, QH), jnp.bfloat16),
        in_specs=[HBM],
        out_specs=VMEM,
        scratch_shapes=[pltpu.SemaphoreType.DMA],
        compiler_params=pltpu.CompilerParams(vmem_limit_bytes=VMEM_LIMIT),
        cost_estimate=pl.CostEstimate(flops=0, bytes_accessed=5000000, transcendentals=0),
        name="fetch",
    )(weights)


def project_kernel(a0, a1, a2, a3, hidden0, hidden1, gate, w, out0, out1, a):
    z_lo, core, b, around, order = places()
    for k, part in enumerate((a0, a1, a2, a3)):
        a[:, pl.ds(pl.multiple_of(around[k] * QH, QH), QH)] = part[...]
    for n in range(2):
        cols = pl.ds(n * QH, QH)
        proj = jnp.dot(a[...], w[n].reshape(HD, QH), preferred_element_type=jnp.float32).astype(jnp.bfloat16)
        for b, (hidden, out) in enumerate(((hidden0, out0), (hidden1, out1))):
            change = gate[b : b + 1, cols] * proj[b * TOK : (b + 1) * TOK, :].astype(jnp.float32)
            out[:, cols] = (hidden[:, cols].astype(jnp.float32) + change).astype(jnp.bfloat16)


def finish_kernel(a0, a1, a2, a3, *rest):
    states, (gate, weights, kept1, kept2, stay, leave, w, a, early, sems) = rest[:8], rest[8:]
    copies = []
    for k, ring in enumerate((0, 1, 3, 2)):
        copies.append(pltpu.make_async_copy(weights.at[:, :, :, pl.ds(ring * 48, 48), :], w.at[k], sems.at[k]))
        copies[-1].start()
    for i, kept in enumerate((kept1, kept2)):

        @pl.when(lax.axis_index("z_lo") == i)
        def bring(kept=kept):
            pltpu.make_async_copy(kept, early, sems.at[4]).start()

    z_lo, core, b, around, order = places()
    for k, part in enumerate((a0, a1, a2, a3)):
        a[:, pl.ds(pl.multiple_of(around[k] * QH, QH), QH)] = part[...]
    pltpu.make_async_copy(kept1, early, sems.at[4]).wait()
    for k in range(4):
        copies[k].wait()
        q = order[k]
        for n in range(2):
            cols = pl.ds(n * QH, QH)
            proj = jnp.dot(a[...], w[k, n].reshape(HD, QH), preferred_element_type=jnp.float32).astype(jnp.bfloat16)
            hidden = jnp.where(b == 0, states[2 * k][:, cols], states[2 * k + 1][:, cols])
            change = gate[q, pl.ds(b, 1), cols] * proj.astype(jnp.float32)
            place = pl.ds(pl.multiple_of(q * QD + n * QH, QH), QH)
            late = jnp.where(z_lo == 0, (hidden.astype(jnp.float32) + change).astype(jnp.bfloat16), hidden)
            stay[:, place] = jnp.where(z_lo == core, late, early[:, place])
            leave[:, place] = jnp.where(z_lo == core, early[:, place], late)


def attention(pieces, mods, tables, weights, first, keeps, last):
    if last:
        attended = (jax.ShapeDtypeStruct((TOK, QH), jnp.bfloat16),) * 2
    else:
        attended = (jax.ShapeDtypeStruct((ROWS, QH), jnp.bfloat16),)
    return pl.pallas_call(
        functools.partial(attention_kernel, first, keeps, last),
        out_shape=attended + (jax.ShapeDtypeStruct((TOK, D), jnp.bfloat16),) * keeps,
        in_specs=[VMEM] * 10 + [HBM],
        out_specs=(VMEM,) * len(attended) + (HBM,) * keeps,
        scratch_shapes=[
            pltpu.VMEM((4, 8, 2, 48, 3 * QH), jnp.bfloat16),
            pltpu.VMEM((ROWS, D), jnp.bfloat16),
            pltpu.VMEM((2, TOK, QH), jnp.bfloat16),
            pltpu.SemaphoreType.DMA((4,)),
            pltpu.SemaphoreType.DMA,
        ],
        compiler_params=pltpu.CompilerParams(vmem_limit_bytes=VMEM_LIMIT),
        cost_estimate=pl.CostEstimate(flops=2 * ROWS * D * 3 * QH, bytes_accessed=10000000, transcendentals=100000),
        name="attention",
    )(*pieces, mods, tables, weights)


def project(parts, hidden, gate, weights):
    return pl.pallas_call(
        project_kernel,
        out_shape=(jax.ShapeDtypeStruct((TOK, QD), jnp.bfloat16),) * 2,
        in_specs=[VMEM] * 8,
        out_specs=(VMEM, VMEM),
        scratch_shapes=[pltpu.VMEM((ROWS, HD), jnp.bfloat16)],
        compiler_params=pltpu.CompilerParams(vmem_limit_bytes=VMEM_LIMIT),
        cost_estimate=pl.CostEstimate(flops=2 * ROWS * HD * QD, bytes_accessed=4000000, transcendentals=0),
        name="project",
    )(*parts, *hidden, gate, weights)


def finish(parts, pieces, gate, weights, kept):
    return pl.pallas_call(
        finish_kernel,
        out_shape=(jax.ShapeDtypeStruct((TOK, D), jnp.bfloat16),) * 2,
        in_specs=[VMEM] * 13 + [HBM] * 3,
        out_specs=(VMEM, VMEM),
        scratch_shapes=[
            pltpu.VMEM((4, 2, 16, 2, 48, QH), jnp.bfloat16),
            pltpu.VMEM((TOK, HD), jnp.bfloat16),
            pltpu.VMEM((TOK, D), jnp.bfloat16),
            pltpu.SemaphoreType.DMA((5,)),
        ],
        compiler_params=pltpu.CompilerParams(vmem_limit_bytes=VMEM_LIMIT),
        cost_estimate=pl.CostEstimate(flops=2 * TOK * HD * D, bytes_accessed=13000000, transcendentals=0),
        name="finish",
    )(*parts, *pieces, gate, weights, *kept)


def pick(options, index):
    return lax.dynamic_index_in_dim(jnp.asarray(options), index, 0, keepdims=False)


def pack_kernel(qkv, outs, packed):
    qkv, outs = qkv[...].T, outs[...].T
    for d in range(32):
        z_hi, plane = d // 16, d % 16
        first, second, last = (2 * plane + z_hi) * 48, (2 * plane + z_hi + 32) * 48, (2 * plane + z_hi) * 48
        packed[d] = jnp.concatenate([qkv[first : first + 48], qkv[second : second + 48], outs[last : last + 48]], axis=1)


def regroup_kernel(mixed, blocks):
    outs = jnp.concatenate([mixed[d, :, 288:384] for d in range(32)], axis=1)
    for c in range(2):
        rows = jnp.concatenate([mixed[d, :, 144 * c : 144 * c + 144] for d in range(32)], axis=1)
        for z in range(4):
            target = (z % 2) * 4 + c * 2 + z // 2
            for j in range(3):
                blocks[target, 48 * j : 48 * j + 48, :] = rows[:, HD * j + QH * z : HD * j + QH * (z + 1)]
            blocks[target, 144:, :] = outs[:, QD * z + QH * c : QD * z + QH * (c + 1)]


def weight_shards(qkv_w, out_w):
    params = pltpu.CompilerParams(vmem_limit_bytes=VMEM_LIMIT)
    packed = pl.pallas_call(
        pack_kernel,
        out_shape=jax.ShapeDtypeStruct((32, 48, 384), jnp.bfloat16),
        compiler_params=params,
        name="pack",
    )(qkv_w.T, out_w.T)
    mixed = lax.all_to_all(packed, ("z_hi", "x", "y"), 0, 0)
    blocks = pl.pallas_call(
        regroup_kernel,
        out_shape=jax.ShapeDtypeStruct((8, 192, QH), jnp.bfloat16),
        compiler_params=params,
        name="regroup",
    )(mixed)
    shards = lax.all_to_all(blocks, ("z_lo", "core", "z_hi"), 0, 0)
    return shards.reshape(LAYERS, 2, 192, QH)


def on_device(latents, modulation, qkv_w, out_w, positions, counts):
    z_lo, core, z_hi = (lax.axis_index(a) for a in ("z_lo", "core", "z_hi"))
    z = 2 * z_hi + z_lo

    small = jnp.zeros((2, 1, D), jnp.float32)
    small = lax.dynamic_update_slice(small, positions.astype(jnp.float32).reshape(2, 1, TOK), (0, 0, 0))
    small = lax.dynamic_update_slice(small, counts.astype(jnp.float32).reshape(2, 1, 1), (0, 0, TOK))
    cond = jnp.concatenate([modulation[0, :, 0], small], axis=1)
    mine = lax.dynamic_index_in_dim(cond, core, 0, keepdims=False)
    theirs = core_swap(lax.dynamic_index_in_dim(cond, 1 - core, 0, keepdims=False))
    pair = jnp.where(core == 0, jnp.stack([mine, theirs]), jnp.stack([theirs, mine]))
    places = [(z - k) % 4 for k in range(4)]
    ring = jnp.stack(ring_gather(pair))
    by_z = [pick(ring, (z - i) % 4) for i in range(4)]
    cond = jnp.stack([jnp.stack([by_z[layer // 2][layer % 2], by_z[2 + layer // 2][layer % 2]]) for layer in range(4)])
    place = cond[0, :, 3, :TOK]
    count = cond[0, :, 3, TOK].astype(jnp.int32)
    mods = cond[:, :, 0:2].reshape(4, 2, 2, 4, QD).transpose(0, 3, 1, 2, 4)
    gates = lax.dynamic_slice_in_dim(cond[:3, :, 2], z * QD, QD, 2)
    last_gate = cond[3, :, 2].reshape(2, 4, QD).transpose(1, 0, 2)

    patch = place.astype(jnp.int32).reshape(ROWS)
    quarter = HSZ // 4
    frequency = 10000.0 ** (-jnp.arange(quarter, dtype=jnp.float32) / quarter)
    row_angle = (patch // GRID).astype(jnp.float32)[:, None] * frequency
    col_angle = (patch % GRID).astype(jnp.float32)[:, None] * frequency
    angle = jnp.concatenate([row_angle, row_angle, col_angle, col_angle], axis=1)
    sine = jnp.sin(angle) * jnp.where(jnp.arange(HSZ) % 64 < 32, -1.0, 1.0).astype(jnp.float32)
    live = jnp.arange(TOK, dtype=jnp.int32) < jnp.repeat(count, TOK)[:, None]
    tables = jnp.stack([jnp.cos(angle), sine, live.astype(jnp.float32)])

    own = lax.dynamic_index_in_dim(latents, core, 0, keepdims=False)[0]
    other = device_permute(own, lambda a, c: (3 - a, c))
    samples = (jnp.where(z_hi == 0, own, other), jnp.where(z_hi == 0, other, own))
    pieces = [sample[:, q * QD : (q + 1) * QD] for q in range(4) for sample in samples]
    quarter_of = [lax.dynamic_slice_in_dim(sample, z * QD, QD, 1) for sample in samples]

    shards = weight_shards(qkv_w[0], out_w[0])
    plane = ("core", "x", "y")
    front = lax.all_gather(jnp.concatenate([shards[0], shards[1]], axis=1), plane)
    middle = lax.all_gather(jnp.concatenate([shards[2], shards[3, :, :144]], axis=1), plane)
    across = jnp.concatenate(ring_gather(shards[3, :, 144:]), axis=1)
    final = lax.all_gather(across, plane)
    front, middle = front.reshape(2, 16, 2, 384, QH), middle.reshape(2, 16, 2, 336, QH)
    final = final.reshape(2, 16, 2, 192, QH)
    weights = [(front, 0), (front, 192), (middle, 0), (middle, 192)]
    kept = []
    for layer in range(LAYERS):
        gathered, first = weights[layer]
        att = attention(pieces, mods[layer], tables, gathered, first, layer in (1, 2), layer == LAYERS - 1)
        if layer in (1, 2):
            *att, keep = att
            kept.append(keep)
        if layer < LAYERS - 1:
            quarter_of = project(ring_gather(att[0]), quarter_of, gates[layer], fetch(gathered, first + 144, att[0]))
            pieces = ring_gather_rows(*quarter_of)

    same, cross = att
    moves = [(cross, {1: 2, 3: 0}), (cross, {0: 2, 2: 0}), (same, {1: 0, 3: 2})]
    parts = [same] + [device_permute(value, lambda a, c: (move[a], c) if a in move else None) for value, move in moves]
    stay, leave = finish(parts, pieces, last_gate, final, kept)
    leave = core_swap(leave)
    first = jnp.where(core == 0, stay, leave)
    second = jnp.where(core == 0, leave, stay)
    return jnp.stack([first, second])[None, :, None]


def solution(mesh):
    ring_mesh = Mesh(mesh.devices.reshape(2, 2, 2, 4, 4), AXES)
    section, dp = ("z_lo", "core"), ("z_hi", "x", "y")
    return jax.shard_map(
        on_device,
        mesh=ring_mesh,
        in_specs=(
            P(None, dp, None, None),
            P(section, None, dp, None, None),
            P(section, None, dp),
            P(section, None, dp),
            P(None, dp, None),
            P(None, dp),
        ),
        out_specs=P(section, None, dp, None, None),
        check_vma=False,
    )
```

```python
import functools

import jax
import jax.numpy as jnp
from jax import lax
from jax.experimental import pallas as pl
from jax.experimental.pallas import tpu as pltpu
from jax.sharding import Mesh
from jax.sharding import PartitionSpec as P

D = 3072
HEADS = 12
HSZ = 128
GRID = 64
TOK = 128
HD = 1536
LAYERS = 4
ROWS = 2 * TOK
QD = D // 4
QH = HD // 4
AXES = ("z_lo", "core", "z_hi", "x", "y")
VMEM_LIMIT = 48 * 1024 * 1024
HBM = pl.BlockSpec(memory_space=pl.ANY)
VMEM = pl.BlockSpec(memory_space=pltpu.VMEM)


def device_permute(value, place):
    pairs = []
    for z in range(4):
        for c in range(2):
            target = place(z, c)
            if target is not None:
                tz, tc = target
                pairs.append(((z % 2) * 4 + c * 2 + z // 2, (tz % 2) * 4 + tc * 2 + tz // 2))
    return lax.ppermute(value, ("z_lo", "core", "z_hi"), pairs)


def ring_step(value, steps):
    return device_permute(value, lambda z, c: ((z + steps) % 4, c))


def ring_gather(value):
    return [value] + [ring_step(value, k) for k in (1, 2, 3)]


def ring_gather_rows(first, second):
    first_before, second_after = ring_step(first, 1), ring_step(second, 3)
    second_before, first_after = ring_step(second, 1), ring_step(first, 3)
    return [first, second, first_before, second_before, first_after, second_after, ring_step(first_before, 1), ring_step(second_after, 3)]


def core_swap(value):
    return lax.ppermute(value, "core", [(0, 1), (1, 0)])


def rotate(values, cosine, sine, first):
    partner = jnp.where(first, pltpu.roll(values, 96, 1), pltpu.roll(values, 32, 1))
    return (values * cosine + partner * sine).astype(jnp.bfloat16)


def places():
    z_lo, core, z_hi = (lax.axis_index(a) for a in ("z_lo", "core", "z_hi"))
    z = 2 * z_hi + z_lo
    around = [lax.rem(z + k, 4) for k in (0, 3, 2, 1)]
    return z_lo, core, z_hi, around, [around[0], around[1], around[3], around[2]]


def attention_kernel(first, keeps, last, *rest):
    _, _, z_hi, _, order = places()
    if not (keeps or last):
        order = [0, 1, 2, 3]
    states, (mods, tables, weights), outs, (w, y, both, sems, keep_sem) = rest[:8], rest[8:11], rest[11:-5], rest[-5:]
    if keeps:
        kept = outs[-1]
        for b in range(2):

            @pl.when(z_hi == b)
            def keep(pieces=states[b::2]):
                for k, p in enumerate(pieces):
                    place = pl.ds(pl.multiple_of(order[k] * QD, QD), QD)
                    pltpu.make_async_copy(p, kept.at[:, place], keep_sem).start()

    for i in range(4):
        core, plane = i // 2, pl.ds(i % 2 * 8, 8)
        for j in range(3):
            source = weights.at[core, plane, :, pl.ds(first + 48 * j, 48), :]
            pltpu.make_async_copy(source, w.at[i, :, :, :, pl.ds(QH * j, QH)], sems.at[i]).start()
    for b in range(2):
        rows = pl.ds(b * TOK, TOK)
        pieces = states[b::2]
        total = jnp.zeros((TOK, 1), jnp.float32)
        for p in pieces:
            total += jnp.sum(p[...].astype(jnp.float32), axis=1, keepdims=True)
        center = total / D
        total = jnp.zeros((TOK, 1), jnp.float32)
        for p in pieces:
            total += jnp.sum((p[...].astype(jnp.float32) - center) ** 2, axis=1, keepdims=True)
        inverse = 1.0 / jnp.sqrt(total / D + 1e-06)
        for k, p in enumerate(pieces):
            q = order[k]
            normed = (p[...].astype(jnp.float32) - center) * inverse
            shift = mods[q, b, 0:1, :]
            scale = mods[q, b, 1:2, :]
            y[rows, pl.ds(pl.multiple_of(q * QD, QD), QD)] = (normed * (1.0 + scale) + shift).astype(jnp.bfloat16)

    total = jnp.zeros((ROWS, 3 * QH), jnp.float32)
    for i in range(4):
        pltpu.make_async_copy(w.at[i], w.at[i], sems.at[i]).wait()
        total += jnp.dot(y[:, i * QD : (i + 1) * QD], w[i].reshape(QD, 3 * QH), preferred_element_type=jnp.float32)
    qkv = total.astype(jnp.bfloat16)
    lane = lax.broadcasted_iota(jnp.int32, (TOK, HSZ), 1)
    first = (lane % 64) < 32
    for b in range(2):
        lo = b * TOK
        cb, sb, live = tables[0, lo : lo + TOK, :], tables[1, lo : lo + TOK, :], tables[2, lo : lo + TOK, :] > 0.0
        for h in range(3):
            query = rotate(qkv[lo : lo + TOK, h * HSZ : (h + 1) * HSZ].astype(jnp.float32), cb, sb, first)
            key = rotate(qkv[lo : lo + TOK, QH + h * HSZ : QH + (h + 1) * HSZ].astype(jnp.float32), cb, sb, first)
            value = qkv[lo : lo + TOK, 2 * QH + h * HSZ : 2 * QH + (h + 1) * HSZ]
            scores = lax.dot_general(query, key, (((1,), (1,)), ((), ())), preferred_element_type=jnp.float32)
            scores = jnp.where(live, scores * HSZ ** (-0.5), -1e30)
            expd = jnp.exp(scores - jnp.max(scores, axis=1, keepdims=True))
            weights = (expd / jnp.sum(expd, axis=1, keepdims=True)).astype(jnp.bfloat16)
            mixed = jnp.dot(weights, value, preferred_element_type=jnp.float32)
            mixed = mixed.astype(jnp.bfloat16)
            cols = pl.ds(h * HSZ, HSZ)
            if last:
                both[b, :, cols] = mixed
            else:
                outs[0][lo : lo + TOK, cols] = mixed
    if last:
        outs[0][...] = both[z_hi]
        outs[1][...] = both[1 - z_hi]
    if keeps:
        pltpu.make_async_copy(kept, kept, keep_sem).wait()


def fetch_kernel(start, weights, out, sem):
    copy = pltpu.make_async_copy(weights.at[:, :, :, pl.ds(start, 48), :], out, sem)
    copy.start()
    copy.wait()


def fetch(weights, start, after):
    weights, _ = lax.optimization_barrier((weights, after))
    return pl.pallas_call(
        functools.partial(fetch_kernel, start),
        out_shape=jax.ShapeDtypeStruct((2, 16, 2, 48, QH), jnp.bfloat16),
        in_specs=[HBM],
        out_specs=VMEM,
        scratch_shapes=[pltpu.SemaphoreType.DMA],
        compiler_params=pltpu.CompilerParams(vmem_limit_bytes=VMEM_LIMIT),
        cost_estimate=pl.CostEstimate(flops=0, bytes_accessed=5000000, transcendentals=0),
        name="fetch",
    )(weights)


def project_kernel(a0, a1, a2, a3, hidden0, hidden1, gate, w, out0, out1, a):
    z_lo, core, b, around, order = places()
    for k, part in enumerate((a0, a1, a2, a3)):
        a[:, pl.ds(pl.multiple_of(around[k] * QH, QH), QH)] = part[...]
    for n in range(2):
        cols = pl.ds(n * QH, QH)
        proj = jnp.dot(a[...], w[n].reshape(HD, QH), preferred_element_type=jnp.float32).astype(jnp.bfloat16)
        for b, (hidden, out) in enumerate(((hidden0, out0), (hidden1, out1))):
            change = gate[b : b + 1, cols] * proj[b * TOK : (b + 1) * TOK, :].astype(jnp.float32)
            out[:, cols] = (hidden[:, cols].astype(jnp.float32) + change).astype(jnp.bfloat16)


def finish_kernel(a0, a1, a2, a3, *rest):
    states, (gate, weights, kept1, kept2, stay, leave, w, a, early, sems) = rest[:8], rest[8:]
    copies = []
    for k, ring in enumerate((0, 1, 3, 2)):
        copies.append(pltpu.make_async_copy(weights.at[:, :, :, pl.ds(ring * 48, 48), :], w.at[k], sems.at[k]))
        copies[-1].start()
    for i, kept in enumerate((kept1, kept2)):

        @pl.when(lax.axis_index("z_lo") == i)
        def bring(kept=kept):
            pltpu.make_async_copy(kept, early, sems.at[4]).start()

    z_lo, core, b, around, order = places()
    for k, part in enumerate((a0, a1, a2, a3)):
        a[:, pl.ds(pl.multiple_of(around[k] * QH, QH), QH)] = part[...]
    pltpu.make_async_copy(kept1, early, sems.at[4]).wait()
    for k in range(4):
        copies[k].wait()
        q = order[k]
        for n in range(2):
            cols = pl.ds(n * QH, QH)
            proj = jnp.dot(a[...], w[k, n].reshape(HD, QH), preferred_element_type=jnp.float32).astype(jnp.bfloat16)
            hidden = jnp.where(b == 0, states[2 * k][:, cols], states[2 * k + 1][:, cols])
            change = gate[q, pl.ds(b, 1), cols] * proj.astype(jnp.float32)
            place = pl.ds(pl.multiple_of(q * QD + n * QH, QH), QH)
            late = jnp.where(z_lo == 0, (hidden.astype(jnp.float32) + change).astype(jnp.bfloat16), hidden)
            stay[:, place] = jnp.where(z_lo == core, late, early[:, place])
            leave[:, place] = jnp.where(z_lo == core, early[:, place], late)


def attention(pieces, mods, tables, weights, first, keeps, last):
    if last:
        attended = (jax.ShapeDtypeStruct((TOK, QH), jnp.bfloat16),) * 2
    else:
        attended = (jax.ShapeDtypeStruct((ROWS, QH), jnp.bfloat16),)
    return pl.pallas_call(
        functools.partial(attention_kernel, first, keeps, last),
        out_shape=attended + (jax.ShapeDtypeStruct((TOK, D), jnp.bfloat16),) * keeps,
        in_specs=[VMEM] * 10 + [HBM],
        out_specs=(VMEM,) * len(attended) + (HBM,) * keeps,
        scratch_shapes=[
            pltpu.VMEM((4, 8, 2, 48, 3 * QH), jnp.bfloat16),
            pltpu.VMEM((ROWS, D), jnp.bfloat16),
            pltpu.VMEM((2, TOK, QH), jnp.bfloat16),
            pltpu.SemaphoreType.DMA((4,)),
            pltpu.SemaphoreType.DMA,
        ],
        compiler_params=pltpu.CompilerParams(vmem_limit_bytes=VMEM_LIMIT),
        cost_estimate=pl.CostEstimate(flops=2 * ROWS * D * 3 * QH, bytes_accessed=10000000, transcendentals=100000),
        name="attention",
    )(*pieces, mods, tables, weights)


def project(parts, hidden, gate, weights):
    return pl.pallas_call(
        project_kernel,
        out_shape=(jax.ShapeDtypeStruct((TOK, QD), jnp.bfloat16),) * 2,
        in_specs=[VMEM] * 8,
        out_specs=(VMEM, VMEM),
        scratch_shapes=[pltpu.VMEM((ROWS, HD), jnp.bfloat16)],
        compiler_params=pltpu.CompilerParams(vmem_limit_bytes=VMEM_LIMIT),
        cost_estimate=pl.CostEstimate(flops=2 * ROWS * HD * QD, bytes_accessed=4000000, transcendentals=0),
        name="project",
    )(*parts, *hidden, gate, weights)


def finish(parts, pieces, gate, weights, kept):
    return pl.pallas_call(
        finish_kernel,
        out_shape=(jax.ShapeDtypeStruct((TOK, D), jnp.bfloat16),) * 2,
        in_specs=[VMEM] * 13 + [HBM] * 3,
        out_specs=(VMEM, VMEM),
        scratch_shapes=[
            pltpu.VMEM((4, 2, 16, 2, 48, QH), jnp.bfloat16),
            pltpu.VMEM((TOK, HD), jnp.bfloat16),
            pltpu.VMEM((TOK, D), jnp.bfloat16),
            pltpu.SemaphoreType.DMA((5,)),
        ],
        compiler_params=pltpu.CompilerParams(vmem_limit_bytes=VMEM_LIMIT),
        cost_estimate=pl.CostEstimate(flops=2 * TOK * HD * D, bytes_accessed=13000000, transcendentals=0),
        name="finish",
    )(*parts, *pieces, gate, weights, *kept)


def pick(options, index):
    return lax.dynamic_index_in_dim(jnp.asarray(options), index, 0, keepdims=False)


def pack_kernel(qkv, outs, packed):
    qkv, outs = qkv[...].T, outs[...].T
    for d in range(32):
        z_hi, plane = d // 16, d % 16
        first, second, last = (2 * plane + z_hi) * 48, (2 * plane + z_hi + 32) * 48, (2 * plane + z_hi) * 48
        packed[d] = jnp.concatenate([qkv[first : first + 48], qkv[second : second + 48], outs[last : last + 48]], axis=1)


def regroup_kernel(mixed, blocks):
    outs = jnp.concatenate([mixed[d, :, 288:384] for d in range(32)], axis=1)
    for c in range(2):
        rows = jnp.concatenate([mixed[d, :, 144 * c : 144 * c + 144] for d in range(32)], axis=1)
        for z in range(4):
            target = (z % 2) * 4 + c * 2 + z // 2
            for j in range(3):
                blocks[target, 48 * j : 48 * j + 48, :] = rows[:, HD * j + QH * z : HD * j + QH * (z + 1)]
            blocks[target, 144:, :] = outs[:, QD * z + QH * c : QD * z + QH * (c + 1)]


def weight_shards(qkv_w, out_w):
    params = pltpu.CompilerParams(vmem_limit_bytes=VMEM_LIMIT)
    packed = pl.pallas_call(
        pack_kernel,
        out_shape=jax.ShapeDtypeStruct((32, 48, 384), jnp.bfloat16),
        compiler_params=params,
        name="pack",
    )(qkv_w.T, out_w.T)
    mixed = lax.all_to_all(packed, ("z_hi", "x", "y"), 0, 0)
    blocks = pl.pallas_call(
        regroup_kernel,
        out_shape=jax.ShapeDtypeStruct((8, 192, QH), jnp.bfloat16),
        compiler_params=params,
        name="regroup",
    )(mixed)
    shards = lax.all_to_all(blocks, ("z_lo", "core", "z_hi"), 0, 0)
    return shards.reshape(LAYERS, 2, 192, QH)


def on_device(latents, modulation, qkv_w, out_w, positions, counts):
    z_lo, core, z_hi = (lax.axis_index(a) for a in ("z_lo", "core", "z_hi"))
    z = 2 * z_hi + z_lo

    small = jnp.zeros((2, 1, D), jnp.float32)
    small = lax.dynamic_update_slice(small, positions.astype(jnp.float32).reshape(2, 1, TOK), (0, 0, 0))
    small = lax.dynamic_update_slice(small, counts.astype(jnp.float32).reshape(2, 1, 1), (0, 0, TOK))
    cond = jnp.concatenate([modulation[0, :, 0], small], axis=1)
    mine = lax.dynamic_index_in_dim(cond, core, 0, keepdims=False)
    theirs = core_swap(lax.dynamic_index_in_dim(cond, 1 - core, 0, keepdims=False))
    pair = jnp.where(core == 0, jnp.stack([mine, theirs]), jnp.stack([theirs, mine]))
    places = [(z - k) % 4 for k in range(4)]
    ring = jnp.stack(ring_gather(pair))
    by_z = [pick(ring, (z - i) % 4) for i in range(4)]
    cond = jnp.stack([jnp.stack([by_z[layer // 2][layer % 2], by_z[2 + layer // 2][layer % 2]]) for layer in range(4)])
    place = cond[0, :, 3, :TOK]
    count = cond[0, :, 3, TOK].astype(jnp.int32)
    mods = cond[:, :, 0:2].reshape(4, 2, 2, 4, QD).transpose(0, 3, 1, 2, 4)
    gates = lax.dynamic_slice_in_dim(cond[:3, :, 2], z * QD, QD, 2)
    last_gate = cond[3, :, 2].reshape(2, 4, QD).transpose(1, 0, 2)

    patch = place.astype(jnp.int32).reshape(ROWS)
    quarter = HSZ // 4
    frequency = 10000.0 ** (-jnp.arange(quarter, dtype=jnp.float32) / quarter)
    row_angle = (patch // GRID).astype(jnp.float32)[:, None] * frequency
    col_angle = (patch % GRID).astype(jnp.float32)[:, None] * frequency
    angle = jnp.concatenate([row_angle, row_angle, col_angle, col_angle], axis=1)
    sine = jnp.sin(angle) * jnp.where(jnp.arange(HSZ) % 64 < 32, -1.0, 1.0).astype(jnp.float32)
    live = jnp.arange(TOK, dtype=jnp.int32) < jnp.repeat(count, TOK)[:, None]
    tables = jnp.stack([jnp.cos(angle), sine, live.astype(jnp.float32)])

    own = lax.dynamic_index_in_dim(latents, core, 0, keepdims=False)[0]
    other = device_permute(own, lambda a, c: (3 - a, c))
    samples = (jnp.where(z_hi == 0, own, other), jnp.where(z_hi == 0, other, own))
    pieces = [sample[:, q * QD : (q + 1) * QD] for q in range(4) for sample in samples]
    quarter_of = [lax.dynamic_slice_in_dim(sample, z * QD, QD, 1) for sample in samples]

    shards = weight_shards(qkv_w[0], out_w[0])
    plane = ("core", "x", "y")
    front = lax.all_gather(jnp.concatenate([shards[0], shards[1]], axis=1), plane)
    middle = lax.all_gather(jnp.concatenate([shards[2], shards[3, :, :144]], axis=1), plane)
    across = jnp.concatenate(ring_gather(shards[3, :, 144:]), axis=1)
    final = lax.all_gather(across, plane)
    front, middle = front.reshape(2, 16, 2, 384, QH), middle.reshape(2, 16, 2, 336, QH)
    final = final.reshape(2, 16, 2, 192, QH)
    weights = [(front, 0), (front, 192), (middle, 0), (middle, 192)]
    kept = []
    for layer in range(LAYERS):
        gathered, first = weights[layer]
        att = attention(pieces, mods[layer], tables, gathered, first, layer in (1, 2), layer == LAYERS - 1)
        if layer in (1, 2):
            *att, keep = att
            kept.append(keep)
        if layer < LAYERS - 1:
            quarter_of = project(ring_gather(att[0]), quarter_of, gates[layer], fetch(gathered, first + 144, att[0]))
            pieces = ring_gather_rows(*quarter_of)

    same, cross = att
    moves = [(cross, {1: 2, 3: 0}), (cross, {0: 2, 2: 0}), (same, {1: 0, 3: 2})]
    parts = [same] + [device_permute(value, lambda a, c: (move[a], c) if a in move else None) for value, move in moves]
    stay, leave = finish(parts, pieces, last_gate, final, kept)
    arrived = core_swap(leave)
    out = lax.dynamic_update_slice(jnp.zeros((2, TOK, D), jnp.bfloat16), stay[None], (core, 0, 0))
    out = lax.dynamic_update_slice(out, arrived[None], (1 - core, 0, 0))
    return out[None, :, None]


def solution(mesh):
    ring_mesh = Mesh(mesh.devices.reshape(2, 2, 2, 4, 4), AXES)
    section, dp = ("z_lo", "core"), ("z_hi", "x", "y")
    return jax.shard_map(
        on_device,
        mesh=ring_mesh,
        in_specs=(
            P(None, dp, None, None),
            P(section, None, dp, None, None),
            P(section, None, dp),
            P(section, None, dp),
            P(None, dp, None),
            P(None, dp),
        ),
        out_specs=P(section, None, dp, None, None),
        check_vma=False,
    )
```

```python
import functools

import jax
import jax.numpy as jnp
from jax import lax
from jax.experimental import pallas as pl
from jax.experimental.pallas import tpu as pltpu
from jax.sharding import Mesh
from jax.sharding import PartitionSpec as P

D = 3072
HEADS = 12
HSZ = 128
GRID = 64
TOK = 128
HD = 1536
LAYERS = 4
ROWS = 2 * TOK
QD = D // 4
QH = HD // 4
AXES = ("z_lo", "core", "z_hi", "x", "y")
VMEM_LIMIT = 48 * 1024 * 1024
HBM = pl.BlockSpec(memory_space=pl.ANY)
VMEM = pl.BlockSpec(memory_space=pltpu.VMEM)


def device_permute(value, place):
    pairs = []
    for z in range(4):
        for c in range(2):
            target = place(z, c)
            if target is not None:
                tz, tc = target
                pairs.append(((z % 2) * 4 + c * 2 + z // 2, (tz % 2) * 4 + tc * 2 + tz // 2))
    return lax.ppermute(value, ("z_lo", "core", "z_hi"), pairs)


def ring_step(value, steps):
    return device_permute(value, lambda z, c: ((z + steps) % 4, c))


def ring_gather(value):
    return [value] + [ring_step(value, k) for k in (1, 2, 3)]


def ring_gather_rows(first, second):
    first_before, second_after = ring_step(first, 1), ring_step(second, 3)
    second_before, first_after = ring_step(second, 1), ring_step(first, 3)
    return [first, second, first_before, second_before, first_after, second_after, ring_step(first_before, 1), ring_step(second_after, 3)]


def core_swap(value):
    return lax.ppermute(value, "core", [(0, 1), (1, 0)])


def rotate(values, cosine, sine, first):
    partner = jnp.where(first, pltpu.roll(values, 96, 1), pltpu.roll(values, 32, 1))
    return (values * cosine + partner * sine).astype(jnp.bfloat16)


def places():
    z_lo, core, z_hi = (lax.axis_index(a) for a in ("z_lo", "core", "z_hi"))
    z = 2 * z_hi + z_lo
    around = [lax.rem(z + k, 4) for k in (0, 3, 2, 1)]
    return z_lo, core, z_hi, around, [around[0], around[1], around[3], around[2]]


def attention_kernel(first, keeps, last, *rest):
    _, _, z_hi, _, order = places()
    if not (keeps or last):
        order = [0, 1, 2, 3]
    states, (mods, tables, weights), outs, (w, y, both, sems, keep_sem) = rest[:8], rest[8:11], rest[11:-5], rest[-5:]
    if keeps:
        kept = outs[-1]
        for b in range(2):

            @pl.when(z_hi == b)
            def keep(pieces=states[b::2]):
                for k, p in enumerate(pieces):
                    place = pl.ds(pl.multiple_of(order[k] * QD, QD), QD)
                    pltpu.make_async_copy(p, kept.at[:, place], keep_sem).start()

    for i in range(4):
        core, plane = i // 2, pl.ds(i % 2 * 8, 8)
        for j in range(3):
            source = weights.at[core, plane, :, pl.ds(first + 48 * j, 48), :]
            pltpu.make_async_copy(source, w.at[i, :, :, :, pl.ds(QH * j, QH)], sems.at[i]).start()
    for b in range(2):
        rows = pl.ds(b * TOK, TOK)
        pieces = states[b::2]
        total = jnp.zeros((TOK, 1), jnp.float32)
        for p in pieces:
            total += jnp.sum(p[...].astype(jnp.float32), axis=1, keepdims=True)
        center = total / D
        total = jnp.zeros((TOK, 1), jnp.float32)
        for p in pieces:
            total += jnp.sum((p[...].astype(jnp.float32) - center) ** 2, axis=1, keepdims=True)
        inverse = 1.0 / jnp.sqrt(total / D + 1e-06)
        for k, p in enumerate(pieces):
            q = order[k]
            normed = (p[...].astype(jnp.float32) - center) * inverse
            shift = mods[q, b, 0:1, :]
            scale = mods[q, b, 1:2, :]
            y[rows, pl.ds(pl.multiple_of(q * QD, QD), QD)] = (normed * (1.0 + scale) + shift).astype(jnp.bfloat16)

    total = jnp.zeros((ROWS, 3 * QH), jnp.float32)
    for i in range(4):
        pltpu.make_async_copy(w.at[i], w.at[i], sems.at[i]).wait()
        total += jnp.dot(y[:, i * QD : (i + 1) * QD], w[i].reshape(QD, 3 * QH), preferred_element_type=jnp.float32)
    qkv = total.astype(jnp.bfloat16)
    lane = lax.broadcasted_iota(jnp.int32, (TOK, HSZ), 1)
    first = (lane % 64) < 32
    for b in range(2):
        lo = b * TOK
        cb, sb, live = tables[0, lo : lo + TOK, :], tables[1, lo : lo + TOK, :], tables[2, lo : lo + TOK, :] > 0.0
        for h in range(3):
            query = rotate(qkv[lo : lo + TOK, h * HSZ : (h + 1) * HSZ].astype(jnp.float32), cb, sb, first)
            key = rotate(qkv[lo : lo + TOK, QH + h * HSZ : QH + (h + 1) * HSZ].astype(jnp.float32), cb, sb, first)
            value = qkv[lo : lo + TOK, 2 * QH + h * HSZ : 2 * QH + (h + 1) * HSZ]
            scores = lax.dot_general(query, key, (((1,), (1,)), ((), ())), preferred_element_type=jnp.float32)
            scores = jnp.where(live, scores * HSZ ** (-0.5), -1e30)
            expd = jnp.exp(scores - jnp.max(scores, axis=1, keepdims=True))
            weights = (expd / jnp.sum(expd, axis=1, keepdims=True)).astype(jnp.bfloat16)
            mixed = jnp.dot(weights, value, preferred_element_type=jnp.float32)
            mixed = mixed.astype(jnp.bfloat16)
            cols = pl.ds(h * HSZ, HSZ)
            if last:
                both[b, :, cols] = mixed
            else:
                outs[0][lo : lo + TOK, cols] = mixed
    if last:
        outs[0][...] = both[z_hi]
        outs[1][...] = both[1 - z_hi]
    if keeps:
        pltpu.make_async_copy(kept, kept, keep_sem).wait()


def fetch_kernel(start, weights, out, sem):
    copy = pltpu.make_async_copy(weights.at[:, :, :, pl.ds(start, 48), :], out, sem)
    copy.start()
    copy.wait()


def fetch(weights, start, after):
    weights, _ = lax.optimization_barrier((weights, after))
    return pl.pallas_call(
        functools.partial(fetch_kernel, start),
        out_shape=jax.ShapeDtypeStruct((2, 16, 2, 48, QH), jnp.bfloat16),
        in_specs=[HBM],
        out_specs=VMEM,
        scratch_shapes=[pltpu.SemaphoreType.DMA],
        compiler_params=pltpu.CompilerParams(vmem_limit_bytes=VMEM_LIMIT),
        cost_estimate=pl.CostEstimate(flops=0, bytes_accessed=5000000, transcendentals=0),
        name="fetch",
    )(weights)


def project_kernel(a0, a1, a2, a3, hidden0, hidden1, gate, w, out0, out1, a):
    z_lo, core, b, around, order = places()
    for k, part in enumerate((a0, a1, a2, a3)):
        a[:, pl.ds(pl.multiple_of(around[k] * QH, QH), QH)] = part[...]
    for n in range(2):
        cols = pl.ds(n * QH, QH)
        proj = jnp.dot(a[...], w[n].reshape(HD, QH), preferred_element_type=jnp.float32).astype(jnp.bfloat16)
        for b, (hidden, out) in enumerate(((hidden0, out0), (hidden1, out1))):
            change = gate[b : b + 1, cols] * proj[b * TOK : (b + 1) * TOK, :].astype(jnp.float32)
            out[:, cols] = (hidden[:, cols].astype(jnp.float32) + change).astype(jnp.bfloat16)


def finish_kernel(a0, a1, a2, a3, *rest):
    states, (gate, weights, kept1, kept2, stay, leave, w, a, early, sems) = rest[:8], rest[8:]
    copies = []
    for k, ring in enumerate((0, 1, 3, 2)):
        for n in range(2):
            source = weights.at[n, :, :, pl.ds(ring * 48, 48), :]
            copies.append(pltpu.make_async_copy(source, w.at[k, n], sems.at[2 * k + n]))
            copies[-1].start()
    for i, kept in enumerate((kept1, kept2)):

        @pl.when(lax.axis_index("z_lo") == i)
        def bring(kept=kept):
            pltpu.make_async_copy(kept, early, sems.at[8]).start()

    z_lo, core, b, around, order = places()
    for k, part in enumerate((a0, a1, a2, a3)):
        a[:, pl.ds(pl.multiple_of(around[k] * QH, QH), QH)] = part[...]
    pltpu.make_async_copy(kept1, early, sems.at[8]).wait()
    for k in range(4):
        q = order[k]
        for n in range(2):
            copies[2 * k + n].wait()
            cols = pl.ds(n * QH, QH)
            proj = jnp.dot(a[...], w[k, n].reshape(HD, QH), preferred_element_type=jnp.float32).astype(jnp.bfloat16)
            hidden = jnp.where(b == 0, states[2 * k][:, cols], states[2 * k + 1][:, cols])
            change = gate[q, pl.ds(b, 1), cols] * proj.astype(jnp.float32)
            place = pl.ds(pl.multiple_of(q * QD + n * QH, QH), QH)
            late = jnp.where(z_lo == 0, (hidden.astype(jnp.float32) + change).astype(jnp.bfloat16), hidden)
            stay[:, place] = jnp.where(z_lo == core, late, early[:, place])
            leave[:, place] = jnp.where(z_lo == core, early[:, place], late)


def attention(pieces, mods, tables, weights, first, keeps, last):
    if last:
        attended = (jax.ShapeDtypeStruct((TOK, QH), jnp.bfloat16),) * 2
    else:
        attended = (jax.ShapeDtypeStruct((ROWS, QH), jnp.bfloat16),)
    return pl.pallas_call(
        functools.partial(attention_kernel, first, keeps, last),
        out_shape=attended + (jax.ShapeDtypeStruct((TOK, D), jnp.bfloat16),) * keeps,
        in_specs=[VMEM] * 10 + [HBM],
        out_specs=(VMEM,) * len(attended) + (HBM,) * keeps,
        scratch_shapes=[
            pltpu.VMEM((4, 8, 2, 48, 3 * QH), jnp.bfloat16),
            pltpu.VMEM((ROWS, D), jnp.bfloat16),
            pltpu.VMEM((2, TOK, QH), jnp.bfloat16),
            pltpu.SemaphoreType.DMA((4,)),
            pltpu.SemaphoreType.DMA,
        ],
        compiler_params=pltpu.CompilerParams(vmem_limit_bytes=VMEM_LIMIT),
        cost_estimate=pl.CostEstimate(flops=2 * ROWS * D * 3 * QH, bytes_accessed=10000000, transcendentals=100000),
        name="attention",
    )(*pieces, mods, tables, weights)


def project(parts, hidden, gate, weights):
    return pl.pallas_call(
        project_kernel,
        out_shape=(jax.ShapeDtypeStruct((TOK, QD), jnp.bfloat16),) * 2,
        in_specs=[VMEM] * 8,
        out_specs=(VMEM, VMEM),
        scratch_shapes=[pltpu.VMEM((ROWS, HD), jnp.bfloat16)],
        compiler_params=pltpu.CompilerParams(vmem_limit_bytes=VMEM_LIMIT),
        cost_estimate=pl.CostEstimate(flops=2 * ROWS * HD * QD, bytes_accessed=4000000, transcendentals=0),
        name="project",
    )(*parts, *hidden, gate, weights)


def finish(parts, pieces, gate, weights, kept):
    return pl.pallas_call(
        finish_kernel,
        out_shape=(jax.ShapeDtypeStruct((TOK, D), jnp.bfloat16),) * 2,
        in_specs=[VMEM] * 13 + [HBM] * 3,
        out_specs=(VMEM, VMEM),
        scratch_shapes=[
            pltpu.VMEM((4, 2, 16, 2, 48, QH), jnp.bfloat16),
            pltpu.VMEM((TOK, HD), jnp.bfloat16),
            pltpu.VMEM((TOK, D), jnp.bfloat16),
            pltpu.SemaphoreType.DMA((9,)),
        ],
        compiler_params=pltpu.CompilerParams(vmem_limit_bytes=VMEM_LIMIT),
        cost_estimate=pl.CostEstimate(flops=2 * TOK * HD * D, bytes_accessed=13000000, transcendentals=0),
        name="finish",
    )(*parts, *pieces, gate, weights, *kept)


def pick(options, index):
    return lax.dynamic_index_in_dim(jnp.asarray(options), index, 0, keepdims=False)


def pack_kernel(qkv, outs, packed):
    qkv, outs = qkv[...].T, outs[...].T
    for d in range(32):
        z_hi, plane = d // 16, d % 16
        first, second, last = (2 * plane + z_hi) * 48, (2 * plane + z_hi + 32) * 48, (2 * plane + z_hi) * 48
        packed[d] = jnp.concatenate([qkv[first : first + 48], qkv[second : second + 48], outs[last : last + 48]], axis=1)


def regroup_kernel(mixed, blocks):
    outs = jnp.concatenate([mixed[d, :, 288:384] for d in range(32)], axis=1)
    for c in range(2):
        rows = jnp.concatenate([mixed[d, :, 144 * c : 144 * c + 144] for d in range(32)], axis=1)
        for z in range(4):
            target = (z % 2) * 4 + c * 2 + z // 2
            for j in range(3):
                blocks[target, 48 * j : 48 * j + 48, :] = rows[:, HD * j + QH * z : HD * j + QH * (z + 1)]
            blocks[target, 144:, :] = outs[:, QD * z + QH * c : QD * z + QH * (c + 1)]


def weight_shards(qkv_w, out_w):
    params = pltpu.CompilerParams(vmem_limit_bytes=VMEM_LIMIT)
    packed = pl.pallas_call(
        pack_kernel,
        out_shape=jax.ShapeDtypeStruct((32, 48, 384), jnp.bfloat16),
        compiler_params=params,
        name="pack",
    )(qkv_w.T, out_w.T)
    mixed = lax.all_to_all(packed, ("z_hi", "x", "y"), 0, 0)
    blocks = pl.pallas_call(
        regroup_kernel,
        out_shape=jax.ShapeDtypeStruct((8, 192, QH), jnp.bfloat16),
        compiler_params=params,
        name="regroup",
    )(mixed)
    shards = lax.all_to_all(blocks, ("z_lo", "core", "z_hi"), 0, 0)
    return shards.reshape(LAYERS, 2, 192, QH)


def on_device(latents, modulation, qkv_w, out_w, positions, counts):
    z_lo, core, z_hi = (lax.axis_index(a) for a in ("z_lo", "core", "z_hi"))
    z = 2 * z_hi + z_lo

    small = jnp.zeros((2, 1, D), jnp.float32)
    small = lax.dynamic_update_slice(small, positions.astype(jnp.float32).reshape(2, 1, TOK), (0, 0, 0))
    small = lax.dynamic_update_slice(small, counts.astype(jnp.float32).reshape(2, 1, 1), (0, 0, TOK))
    cond = jnp.concatenate([modulation[0, :, 0], small], axis=1)
    mine = lax.dynamic_index_in_dim(cond, core, 0, keepdims=False)
    theirs = core_swap(lax.dynamic_index_in_dim(cond, 1 - core, 0, keepdims=False))
    pair = jnp.where(core == 0, jnp.stack([mine, theirs]), jnp.stack([theirs, mine]))
    places = [(z - k) % 4 for k in range(4)]
    ring = jnp.stack(ring_gather(pair))
    by_z = [pick(ring, (z - i) % 4) for i in range(4)]
    cond = jnp.stack([jnp.stack([by_z[layer // 2][layer % 2], by_z[2 + layer // 2][layer % 2]]) for layer in range(4)])
    place = cond[0, :, 3, :TOK]
    count = cond[0, :, 3, TOK].astype(jnp.int32)
    mods = cond[:, :, 0:2].reshape(4, 2, 2, 4, QD).transpose(0, 3, 1, 2, 4)
    gates = lax.dynamic_slice_in_dim(cond[:3, :, 2], z * QD, QD, 2)
    last_gate = cond[3, :, 2].reshape(2, 4, QD).transpose(1, 0, 2)

    patch = place.astype(jnp.int32).reshape(ROWS)
    quarter = HSZ // 4
    frequency = 10000.0 ** (-jnp.arange(quarter, dtype=jnp.float32) / quarter)
    row_angle = (patch // GRID).astype(jnp.float32)[:, None] * frequency
    col_angle = (patch % GRID).astype(jnp.float32)[:, None] * frequency
    angle = jnp.concatenate([row_angle, row_angle, col_angle, col_angle], axis=1)
    sine = jnp.sin(angle) * jnp.where(jnp.arange(HSZ) % 64 < 32, -1.0, 1.0).astype(jnp.float32)
    live = jnp.arange(TOK, dtype=jnp.int32) < jnp.repeat(count, TOK)[:, None]
    tables = jnp.stack([jnp.cos(angle), sine, live.astype(jnp.float32)])

    own = lax.dynamic_index_in_dim(latents, core, 0, keepdims=False)[0]
    other = device_permute(own, lambda a, c: (3 - a, c))
    samples = (jnp.where(z_hi == 0, own, other), jnp.where(z_hi == 0, other, own))
    pieces = [sample[:, q * QD : (q + 1) * QD] for q in range(4) for sample in samples]
    quarter_of = [lax.dynamic_slice_in_dim(sample, z * QD, QD, 1) for sample in samples]

    shards = weight_shards(qkv_w[0], out_w[0])
    plane = ("core", "x", "y")
    front = lax.all_gather(jnp.concatenate([shards[0], shards[1]], axis=1), plane)
    middle = lax.all_gather(jnp.concatenate([shards[2], shards[3, :, :144]], axis=1), plane)
    across = jnp.concatenate(ring_gather(shards[3, :, 144:]), axis=1)
    final = lax.all_gather(across, plane)
    front, middle = front.reshape(2, 16, 2, 384, QH), middle.reshape(2, 16, 2, 336, QH)
    final = final.reshape(2, 16, 2, 192, QH)
    weights = [(front, 0), (front, 192), (middle, 0), (middle, 192)]
    kept = []
    for layer in range(LAYERS):
        gathered, first = weights[layer]
        att = attention(pieces, mods[layer], tables, gathered, first, layer in (1, 2), layer == LAYERS - 1)
        if layer in (1, 2):
            *att, keep = att
            kept.append(keep)
        if layer < LAYERS - 1:
            quarter_of = project(ring_gather(att[0]), quarter_of, gates[layer], fetch(gathered, first + 144, att[0]))
            pieces = ring_gather_rows(*quarter_of)

    same, cross = att
    moves = [(cross, {1: 2, 3: 0}), (cross, {0: 2, 2: 0}), (same, {1: 0, 3: 2})]
    parts = [same] + [device_permute(value, lambda a, c: (move[a], c) if a in move else None) for value, move in moves]
    stay, leave = finish(parts, pieces, last_gate, final, kept)
    arrived = core_swap(leave)
    out = lax.dynamic_update_slice(jnp.zeros((2, TOK, D), jnp.bfloat16), stay[None], (core, 0, 0))
    out = lax.dynamic_update_slice(out, arrived[None], (1 - core, 0, 0))
    return out[None, :, None]


def solution(mesh):
    ring_mesh = Mesh(mesh.devices.reshape(2, 2, 2, 4, 4), AXES)
    section, dp = ("z_lo", "core"), ("z_hi", "x", "y")
    return jax.shard_map(
        on_device,
        mesh=ring_mesh,
        in_specs=(
            P(None, dp, None, None),
            P(section, None, dp, None, None),
            P(section, None, dp),
            P(section, None, dp),
            P(None, dp, None),
            P(None, dp),
        ),
        out_specs=P(section, None, dp, None, None),
        check_vma=False,
    )
```
